256 devices in a mesh: outer: 16 (over y_hi, x, core), inner: 16 (over y_lo, z).
Axes of the slice: x: 4, y: 4 (y_hi: 2, y_lo: 2; y = y_hi * 2 + y_lo), z: 8, core: 2. Of those that a mesh axis runs over, the one named last changes fastest.
Arguments:
- images: bfloat16 [32768, 384], P(('outer', 'inner')), may hold values from -4 to 4
- texts: bfloat16 [32768, 384], P(('outer', 'inner')), may hold values from -4 to 4
- logit_scale: float32 [1], replicated, may hold values from 8 to 16
Outputs:
- loss: float32 [1], replicated
- grad_image: float32 [32768, 384], P(('outer', 'inner'))
- grad_text: float32 [32768, 384], P(('outer', 'inner'))
The draws below stay inside these ranges and needn't reach their ends.
All inputs are finite; a program needn't handle non-finite values.
Results may differ from the reference program's by a relative error of at most 0.0018.
Values may be sent and summed in bfloat16 or wider, within the bound.
A program may use at most 64 MiB of HBM per device.

```python
import math
import jax
import jax.numpy as jnp
from jax import lax

E = 384
PAIRS = 32768
N_OUTER = 16


def rough_rows(key_values, key_factors, low, high):
    raw = jax.random.normal(key_values, (PAIRS, E), jnp.float32)
    factors = jnp.exp(jax.random.uniform(key_factors, (PAIRS, 1), jnp.float32, math.log(low), math.log(high)))
    return raw * factors * 0.5 * E ** (-0.25)


def draw_images(key, part):
    key = jax.random.fold_in(key, 1)
    first, second = jax.random.split(key, 2)
    values = rough_rows(first, second, 0.4, 4.0)
    return jnp.clip(values, -4.0, 4.0).astype(jnp.bfloat16)


def draw_texts(key, part):
    key = jax.random.fold_in(key, 2)
    first, second = jax.random.split(key, 2)
    values = rough_rows(first, second, 0.4, 4.0)
    return jnp.clip(values, -4.0, 4.0).astype(jnp.bfloat16)


def setup_inputs(seed: int = 0) -> dict:
    arg_keys = jax.random.split(jax.random.key(seed), 4)
    images = draw_images(jax.random.fold_in(arg_keys[3], 71), 0)
    texts = draw_texts(jax.random.fold_in(arg_keys[3], 71), 0)
    logit_scale = jnp.clip(jnp.exp(jax.random.uniform(arg_keys[2], (1,), jnp.float32, math.log(8.0), math.log(16.0))), 8.0, 16.0)
    return dict(images=images, texts=texts, logit_scale=logit_scale)


def reference(images, texts, logit_scale):
    factor = logit_scale[0]
    block_count = N_OUTER
    block_width = PAIRS // block_count
    image_blocks = images.reshape(block_count, block_width, E)

    def stats_advance(carry, image_block):
        column_max, column_sum = carry
        score_tile = factor * jnp.dot(image_block, texts.T, preferred_element_type=jnp.float32)
        row_max = score_tile.max(1)
        row_lse = row_max + jnp.log(jnp.sum(jnp.exp(score_tile - row_max[:, None]), 1))
        new_max = jnp.maximum(column_max, score_tile.max(0))
        column_sum = column_sum * jnp.exp(column_max - new_max) + jnp.sum(jnp.exp(score_tile - new_max[None, :]), 0)
        return (new_max, column_sum), row_lse

    initial = (jnp.full((PAIRS,), -1e30, jnp.float32), jnp.zeros((PAIRS,), jnp.float32))
    (column_max, column_sum), row_blocks = lax.scan(stats_advance, initial, image_blocks)
    lse_row = row_blocks.reshape(PAIRS)
    lse_col = column_max + jnp.log(column_sum)
    diagonal = factor * jnp.sum(images.astype(jnp.float32) * texts.astype(jnp.float32), 1)
    loss = ((jnp.sum(lse_row) + jnp.sum(lse_col) - 2.0 * jnp.sum(diagonal)) / (2.0 * PAIRS)).reshape(1)

    def grad_advance(text_total, inputs):
        image_block, block_lse = inputs
        score_tile = factor * jnp.dot(image_block, texts.T, preferred_element_type=jnp.float32)
        weights = ((jnp.exp(score_tile - block_lse[:, None]) + jnp.exp(score_tile - lse_col[None, :])) * 0.5).astype(jnp.bfloat16)
        image_part = jnp.dot(weights, texts, preferred_element_type=jnp.float32)
        text_total = text_total + jnp.dot(weights.T, image_block, preferred_element_type=jnp.float32)
        return text_total, image_part

    text_total, image_parts = lax.scan(grad_advance, jnp.zeros((PAIRS, E), jnp.float32), (image_blocks, row_blocks))
    image_total = image_parts.reshape(PAIRS, E)
    grad_image = factor * (image_total - texts.astype(jnp.float32))
    grad_text = factor * (text_total - images.astype(jnp.float32))
    return loss, grad_image, grad_text
```

```python
import math

import jax
import jax.numpy as jnp
from jax import lax
from jax.experimental import pallas as pl
from jax.experimental.pallas import tpu as pltpu
from jax.sharding import PartitionSpec as P

MESH = pl.DeviceIdType.MESH
F32 = jnp.float32
BF16 = jnp.bfloat16
B = 128
E = 384
NX, NY, NZ = 4, 4, 8
ROWS = NZ * 2 * B
COLS = NX * NY * B
R2 = 2 * B
LOG2E = math.log2(math.e)
LN2 = math.log(2.0)


def nt(a, b):
    return lax.dot_general(a, b, (((1,), (1,)), ((), ())), preferred_element_type=F32)


def kernel(
    scale_ref, img_ref, txt_ref, loss_ref, gi_ref, gt_ref,
    img_all, txt_all, img_t, s_ref, w_ref,
    rm_ref, rl_ref, cm_ref, cl_ref, lrb_ref, lc_ref,
    msg_r, msg_c, got_r, got_c, out_a, out_b, got_a, got_b,
    keep_i, sib_out, sib_in, far_out, far_in, keep_t, t_out, t_in,
    is_s, is_r, fs_s, fs_r, ts_s, ts_r, mr_s, mr_r, mc_s, mc_r,
    la_s, la_r, lb_s, lb_r, sb_s, sb_r, fo_s, fo_r, to_s, to_r,
):
    outer, inner = lax.axis_index("outer"), lax.axis_index("inner")
    c = outer % 2
    x = (outer // 2) % NX
    y = (outer // (2 * NX)) * 2 + inner // NZ
    z = inner % NZ
    factor = scale_ref[0]
    f2 = factor * LOG2E

    def dev(dx, dy, dz, dc):
        xx, yy, zz = (x + dx + NX) % NX, (y + dy + NY) % NY, (z + dz + NZ) % NZ
        cc = (c + dc) % 2
        return ((yy // 2) * (2 * NX) + xx * 2 + cc, (yy % 2) * NZ + zz)

    def rcopy(src, dst, ss, rs, to):
        return pltpu.make_async_remote_copy(
            src_ref=src, dst_ref=dst, send_sem=ss, recv_sem=rs, device_id=to, device_id_type=MESH
        )

    barrier = pltpu.get_barrier_semaphore()
    row_peers = [(d, r) for d in range(NZ) for r in range(2) if (d, r) != (0, 0)]
    col_peers = [(i, j) for i in range(NX) for j in range(NY) if (i, j) != (0, 0)]
    for d, r in row_peers:
        pl.semaphore_signal(barrier, inc=1, device_id=dev(0, 0, d, r), device_id_type=MESH)
    for i, j in col_peers:
        pl.semaphore_signal(barrier, inc=1, device_id=dev(i, j, 0, 0), device_id_type=MESH)
    pl.semaphore_wait(barrier, len(row_peers) + len(col_peers))

    def img_copy(k):
        return rcopy(img_ref, img_all.at[pl.ds(k * R2, B)], is_s.at[k], is_r.at[k], dev(0, 0, k, 0))

    def sib_copy(k):
        return rcopy(
            img_all.at[pl.ds(k * R2, B)], img_all.at[pl.ds(k * R2 + B, B)], fs_s.at[k], fs_r.at[k], dev(0, 0, 0, 1)
        )

    def txt_copy(i, j):
        q = i * NY + j
        return rcopy(txt_ref, txt_all.at[pl.ds(q * B, B)], ts_s.at[q], ts_r.at[q], dev(i, j, 0, 0))

    img_all[0:B, :] = img_ref[...]
    txt_all[0:B, :] = txt_ref[...]
    sib_copy(0).start()
    for k in (1, 7, 2, 6, 3, 5, 4):
        img_copy(k).start()
    for i, j in col_peers:
        txt_copy(i, j).start()

    prod = img_ref[...].astype(F32) * txt_ref[...].astype(F32)
    prod = prod[:, 0:128] + prod[:, 128:256] + prod[:, 256:384]
    msg_r[16:24, :] = jnp.sum(prod.reshape(B // 8, 8, 128), 0)

    for i, j in col_peers:
        txt_copy(i, j).wait()

    def first_step(n, _):
        k = jnp.where(n % 2 == 1, (n + 1) // 2, (NZ - n // 2) % NZ)
        row0 = pl.multiple_of(k * R2, R2)

        @pl.when(n > 0)
        def _():
            img_copy(k).wait()
            sib_copy(k).start()

        sib_copy(k).wait()
        block = img_all[pl.ds(row0, R2), :]
        img_t[:, pl.ds(row0, R2)] = block.T
        for cc in range(COLS // 256):
            s = nt(block, txt_all[cc * 256 : (cc + 1) * 256, :]) * f2
            s_ref[pl.ds(row0, R2), cc * 256 : (cc + 1) * 256] = s
        for cc in range(COLS // 128):
            lanes = slice(cc * 128, (cc + 1) * 128)
            slab = s_ref[pl.ds(row0, R2), lanes].reshape(R2 // 8, 8, 128)
            top = jnp.max(slab, 0)
            cm_ref[k, :, lanes] = top
            cl_ref[k, :, lanes] = jnp.sum(jnp.exp2(slab - top[None]), 0)
        for rr in range(R2 // 16):
            rows = pl.ds(row0 + rr * 16, 16)
            parts = [s_ref[rows, cc * 128 : (cc + 1) * 128] for cc in range(COLS // 128)]
            top = parts[0]
            for p in parts[1:]:
                top = jnp.maximum(top, p)
            total = jnp.exp2(parts[0] - top)
            for p in parts[1:]:
                total = total + jnp.exp2(p - top)
            rm_ref[rr * 16 : rr * 16 + 16, :] = top
            rl_ref[rr * 16 : rr * 16 + 16, :] = total
        for r in range(2):
            mt = rm_ref[r * B : (r + 1) * B, :].T
            lt = rl_ref[r * B : (r + 1) * B, :].T
            top = jnp.max(mt, 0, keepdims=True)
            total = jnp.sum(lt * jnp.exp2(mt - top), 0, keepdims=True)
            msg_r[pl.ds(r * NZ + k, 1), :] = top + jnp.log(total) * LOG2E
        return 0

    lax.fori_loop(0, NZ, first_step, 0)

    for cc in range(COLS // 128):
        lanes = slice(cc * 128, (cc + 1) * 128)
        mt = cm_ref[:, :, lanes].reshape(NZ * 8, 128)
        lt = cl_ref[:, :, lanes].reshape(NZ * 8, 128)
        top = jnp.max(mt, 0, keepdims=True)
        total = jnp.sum(lt * jnp.exp2(mt - top), 0, keepdims=True)
        msg_c[cc : cc + 1, :] = top + jnp.log(total) * LOG2E

    def row_msg(d, r):
        q = d * 2 + r
        return rcopy(msg_r, got_r.at[q], mr_s.at[q], mr_r.at[q], dev(0, 0, d, r))

    def col_msg(i, j):
        q = i * NY + j
        return rcopy(msg_c, got_c.at[q], mc_s.at[q], mc_r.at[q], dev(i, j, 0, 0))

    for d, r in row_peers:
        row_msg(d, r).start()
    for i, j in col_peers:
        col_msg(i, j).start()

    def combine(parts):
        top = parts[0]
        for p in parts[1:]:
            top = jnp.maximum(top, p)
        total = jnp.exp2(parts[0] - top)
        for p in parts[1:]:
            total = total + jnp.exp2(p - top)
        return top + jnp.log(total) * LOG2E

    for d, r in row_peers:
        row_msg(d, r).wait()
    halves = ([], [])
    diag = msg_r[16:24, :]
    for d in range(NZ):
        for r in range(2):
            ref = msg_r if (d, r) == (0, 0) else got_r.at[d * 2 + r]
            if (d, r) != (0, 0):
                diag = diag + ref[16:24, :]
            for rs in range(2):
                v = ref[rs * 8 : rs * 8 + 8, :]
                halves[rs ^ r].append(pltpu.roll(v, d, 0) if d else v)
    lr = [combine(h) for h in halves]

    for i, j in col_peers:
        col_msg(i, j).wait()
    jj = lax.broadcasted_iota(jnp.int32, (NX * NY, 128), 0) % NY
    parts = []
    for a in range(NX):
        for b in range(NY):
            v = msg_c[...] if (a, b) == (0, 0) else got_c[a * NY + b]
            s1, s2 = (4 * a + b) % 16, (4 * a + b + 12) % 16
            if b == 0:
                v = pltpu.roll(v, s1, 0) if s1 else v
            else:
                v = jnp.where(jj >= b, pltpu.roll(v, s1, 0), pltpu.roll(v, s2, 0) if s2 else v)
            parts.append(v)
    lc = combine(parts)
    lc_ref[...] = lc + 1.0

    out_a[...] = (lr[0] + lr[1]) * LN2 - (2.0 * factor) * diag
    out_b[...] = (lc[0:8] + lc[8:16]) * LN2

    def a_msg(i, j):
        q = i * NY + j
        return rcopy(out_a, got_a.at[q], la_s.at[q], la_r.at[q], dev(i, j, 0, 0))

    def b_msg(d, r):
        q = d * 2 + r
        return rcopy(out_b, got_b.at[q], lb_s.at[q], lb_r.at[q], dev(0, 0, d, r))

    for i, j in col_peers:
        a_msg(i, j).start()
    for d, r in row_peers:
        b_msg(d, r).start()

    for k in range(NZ):
        for r in range(2):
            lrb_ref[k * R2 + r * B : k * R2 + (r + 1) * B, :] = (
                jnp.broadcast_to(lr[r][k : k + 1, :], (B, 128)) + 1.0
            ).T

    def order(n):
        return jnp.where(n % 2 == 0, NZ // 2 - n // 2, (NZ // 2 + (n + 1) // 2) % NZ)

    def sib_part(k):
        return rcopy(sib_out.at[k], sib_in.at[k], sb_s.at[k], sb_r.at[k], dev(0, 0, 0, 1))

    def far_part(k):
        return rcopy(far_out.at[k], far_in.at[k], fo_s.at[k], fo_r.at[k], dev(0, 0, -k, 0))

    def pass_on(k):
        sib_part(k).wait_recv()
        far_out[k] = (keep_i[k] + sib_in[k]).astype(BF16)
        far_part(k).start()

    def second_step(n, _):
        k = order(n)
        row0 = pl.multiple_of(k * R2, R2)
        rows = pl.ds(row0, R2)
        for cc in range(COLS // 128):
            lanes = slice(cc * 128, (cc + 1) * 128)
            s = s_ref[rows, lanes]
            w = jnp.exp2(s - lrb_ref[rows, :]) + jnp.exp2(s - lc_ref[cc : cc + 1, :])
            w_ref[rows, lanes] = w.astype(BF16)
        part = jnp.dot(w_ref[rows, :], txt_all[...], preferred_element_type=F32)
        keep_i[k] = part[0:B]
        sib_out[k] = part[B:R2]
        sib_part(k).start()

        @pl.when(n > 0)
        def _():
            pass_on(order(n - 1))

        return 0

    lax.fori_loop(0, NZ, second_step, 0)

    def txt_part(q):
        i, j = q // NY, q % NY
        return rcopy(t_out.at[q], t_in.at[q], to_s.at[q], to_r.at[q], dev(-i, -j, 0, 0))

    def third(cc):
        return jnp.dot(img_t[...], w_ref[:, pl.ds(pl.multiple_of(cc * 256, 256), 256)], preferred_element_type=F32)

    def third_step(n, _):
        cc = COLS // 256 - 1 - n
        part = third(cc)
        for h in range(2):
            t_out[2 * cc + h] = part[:, h * 128 : (h + 1) * 128].astype(BF16)
            txt_part(2 * cc + h).start()
        return 0

    lax.fori_loop(0, COLS // 256 - 1, third_step, 0)
    part = third(0)
    keep_t[...] = part[:, 0:128]
    t_out[1] = part[:, 128:256].astype(BF16)
    txt_part(1).start()

    sib_part(0).wait_recv()
    total = keep_i[0] + sib_in[0]
    for k in range(1, NZ):
        far_part(k).wait_recv()
        total = total + far_in[k].astype(F32)
    gi_ref[...] = factor * (total - txt_ref[...].astype(F32))

    for i, j in col_peers:
        a_msg(i, j).wait()
    for d, r in row_peers:
        b_msg(d, r).wait()
    share = out_a[...] + out_b[...]
    for q in range(1, 16):
        share = share + got_a[q] + got_b[q]
    loss_ref[0] = jnp.sum(share) / (2.0 * 256 * B)

    total = keep_t[...]
    for q in range(1, 16):
        txt_part(q).wait_recv()
        total = total + t_in[q].astype(F32)
    gt_ref[...] = factor * (total.T - img_ref[...].astype(F32))

    for k in range(NZ):
        sib_part(k).wait_send()
    for k in range(1, NZ):
        far_part(k).wait_send()
    for q in range(1, 16):
        txt_part(q).wait_send()


def local(images, texts, logit_scale):
    dma = pltpu.SemaphoreType.DMA
    vm = pltpu.VMEM
    return pl.pallas_call(
        kernel,
        out_shape=(
            jax.ShapeDtypeStruct((1,), F32),
            jax.ShapeDtypeStruct((B, E), F32),
            jax.ShapeDtypeStruct((B, E), F32),
        ),
        in_specs=[
            pl.BlockSpec(memory_space=pltpu.SMEM),
            pl.BlockSpec(memory_space=vm),
            pl.BlockSpec(memory_space=vm),
        ],
        out_specs=(
            pl.BlockSpec(memory_space=pltpu.SMEM),
            pl.BlockSpec(memory_space=vm),
            pl.BlockSpec(memory_space=vm),
        ),
        scratch_shapes=[
            vm((ROWS, E), BF16), vm((COLS, E), BF16), vm((E, ROWS), BF16),
            vm((ROWS, COLS), F32), vm((ROWS, COLS), BF16),
            vm((R2, 128), F32), vm((R2, 128), F32), vm((NZ, 8, COLS), F32), vm((NZ, 8, COLS), F32),
            vm((ROWS, 128), F32), vm((16, 128), F32),
            vm((24, 128), F32), vm((16, 128), F32), vm((16, 24, 128), F32), vm((16, 16, 128), F32),
            vm((8, 128), F32), vm((8, 128), F32), vm((16, 8, 128), F32), vm((16, 8, 128), F32),
            vm((NZ, B, E), F32), vm((NZ, B, E), F32), vm((NZ, B, E), F32),
            vm((NZ, B, E), BF16), vm((NZ, B, E), BF16),
            vm((E, B), F32), vm((16, E, B), BF16), vm((16, E, B), BF16),
            dma((NZ,)), dma((NZ,)), dma((NZ,)), dma((NZ,)), dma((16,)), dma((16,)),
            dma((16,)), dma((16,)), dma((16,)), dma((16,)),
            dma((16,)), dma((16,)), dma((16,)), dma((16,)),
            dma((NZ,)), dma((NZ,)), dma((NZ,)), dma((NZ,)), dma((16,)), dma((16,)),
        ],
        compiler_params=pltpu.CompilerParams(
            collective_id=0, has_side_effects=True, vmem_limit_bytes=56 * 1024 * 1024
        ),
        cost_estimate=pl.CostEstimate(
            flops=6 * ROWS * COLS * E, bytes_accessed=8 * B * E, transcendentals=4 * ROWS * COLS
        ),
    )(logit_scale, images, texts)


def solution(mesh):
    spec = P(("outer", "inner"), None)
    return jax.shard_map(
        local, mesh=mesh, in_specs=(spec, spec, P()), out_specs=(P(), spec, spec), check_vma=False
    )
```

```python
import math

import jax
import jax.numpy as jnp
from jax import lax
from jax.experimental import pallas as pl
from jax.experimental.pallas import tpu as pltpu
from jax.sharding import PartitionSpec as P

MESH = pl.DeviceIdType.MESH
F32 = jnp.float32
BF16 = jnp.bfloat16
B = 128
E = 384
NX, NY, NZ = 4, 4, 8
ROWS = NZ * 2 * B
COLS = NX * NY * B
R2 = 2 * B
QC = 4 * B
LOG2E = math.log2(math.e)
LN2 = math.log(2.0)


def nt(a, b):
    return lax.dot_general(a, b, (((1,), (1,)), ((), ())), preferred_element_type=F32)


def kernel(
    scale_ref, img_ref, txt_ref, loss_ref, gi_ref, gt_ref,
    img_all, txt_all, img_t, s_ref, w_ref,
    rm_ref, rl_ref, cm_ref, cl_ref, lrb_ref, lc_ref,
    msg_r, msg_c, got_r, got_c, out_a, out_b, got_a, got_b,
    keep_i, sib_out, sib_in, far_out, far_in, keep_t, t_out, t_in,
    is_s, is_r, fs_s, fs_r, ts_s, ts_r, mr_s, mr_r, mc_s, mc_r,
    la_s, la_r, lb_s, lb_r, sb_s, sb_r, fo_s, fo_r, to_s, to_r,
):
    outer, inner = lax.axis_index("outer"), lax.axis_index("inner")
    c = outer % 2
    x = (outer // 2) % NX
    y = (outer // (2 * NX)) * 2 + inner // NZ
    z = inner % NZ
    factor = scale_ref[0]
    f2 = factor * LOG2E

    def dev(dx, dy, dz, dc):
        xx, yy, zz = (x + dx + NX) % NX, (y + dy + NY) % NY, (z + dz + NZ) % NZ
        cc = (c + dc) % 2
        return ((yy // 2) * (2 * NX) + xx * 2 + cc, (yy % 2) * NZ + zz)

    def dev_ab(da, db):
        return dev(jnp.where(c == 0, da, db), jnp.where(c == 0, db, da), 0, 0)

    def rcopy(src, dst, ss, rs, to):
        return pltpu.make_async_remote_copy(
            src_ref=src, dst_ref=dst, send_sem=ss, recv_sem=rs, device_id=to, device_id_type=MESH
        )

    barrier = pltpu.get_barrier_semaphore()
    row_peers = [(d, r) for d in range(NZ) for r in range(2) if (d, r) != (0, 0)]
    col_peers = [(i, j) for i in range(NX) for j in range(NY) if (i, j) != (0, 0)]
    for d, r in row_peers:
        pl.semaphore_signal(barrier, inc=1, device_id=dev(0, 0, d, r), device_id_type=MESH)
    for i, j in col_peers:
        pl.semaphore_signal(barrier, inc=1, device_id=dev_ab(i, j), device_id_type=MESH)
    pl.semaphore_wait(barrier, len(row_peers) + len(col_peers))

    def img_rows(k, h=None):
        return img_all.at[pl.ds(k * R2, B)] if h is None else img_all.at[pl.ds(k * R2 + h * 64, 64)]

    def img_copy(k):
        return rcopy(img_ref, img_rows(k), is_s.at[k], is_r.at[k], dev(0, 0, k, 0))

    def img_forward(k, h=None):
        if k == 3:
            return rcopy(img_rows(2), img_rows(3), is_s.at[3], is_r.at[3], dev(0, 0, 1, 0))
        if k == 5:
            return rcopy(img_rows(6), img_rows(5), is_s.at[5], is_r.at[5], dev(0, 0, -1, 0))
        if h == 0:
            return rcopy(img_rows(2, 0), img_rows(4, 0), is_s.at[4], is_r.at[4], dev(0, 0, 2, 0))
        return rcopy(img_rows(6, 1), img_rows(4, 1), is_s.at[8], is_r.at[8], dev(0, 0, -2, 0))

    def sib_copy(k):
        return rcopy(img_rows(k), img_all.at[pl.ds(k * R2 + B, B)], fs_s.at[k], fs_r.at[k], dev(0, 0, 0, 1))

    def txt_first(i):
        return rcopy(txt_ref, txt_all.at[pl.ds(i * B, B)], ts_s.at[i], ts_r.at[i], dev_ab(i, 0))

    def txt_second(j):
        return rcopy(
            txt_all.at[pl.ds(0, QC)], txt_all.at[pl.ds(j * QC, QC)], ts_s.at[3 + j], ts_r.at[3 + j], dev_ab(0, j)
        )

    img_all[0:B, :] = img_ref[...]
    txt_all[0:B, :] = txt_ref[...]
    for i in (1, 3, 2):
        txt_first(i).start()
    for k in (2, 6, 1, 7):
        img_copy(k).start()
    sib_copy(0).start()

    prod = img_ref[...].astype(F32) * txt_ref[...].astype(F32)
    prod = prod[:, 0:128] + prod[:, 128:256] + prod[:, 256:384]
    msg_r[16:24, :] = jnp.sum(prod.reshape(B // 8, 8, 128), 0)

    def near(n):
        return jnp.where(n % 2 == 1, (n + 1) // 2, (NZ - n // 2) % NZ)

    def tile(k, j):
        row0 = pl.multiple_of(k * R2, R2)
        block = img_all[pl.ds(row0, R2), :]
        for cc in range(j * 2, j * 2 + 2):
            s = nt(block, txt_all[cc * 256 : (cc + 1) * 256, :]) * f2
            s_ref[pl.ds(row0, R2), cc * 256 : (cc + 1) * 256] = s
        for cc in range(j * 4, j * 4 + 4):
            lanes = slice(cc * 128, (cc + 1) * 128)
            slab = s_ref[pl.ds(row0, R2), lanes].reshape(R2 // 8, 8, 128)
            top = jnp.max(slab, 0)
            cm_ref[k, :, lanes] = top
            cl_ref[k, :, lanes] = jnp.sum(jnp.exp2(slab - top[None]), 0)
        for rr in range(R2 // 32):
            rows = pl.ds(row0 + rr * 32, 32)
            parts = [s_ref[rows, cc * 128 : (cc + 1) * 128] for cc in range(j * 4, j * 4 + 4)]
            top = jnp.maximum(jnp.maximum(parts[0], parts[1]), jnp.maximum(parts[2], parts[3]))
            e = [jnp.exp2(p - top) for p in parts]
            rm_ref[j, rows, :] = top
            rl_ref[j, rows, :] = (e[0] + e[1]) + (e[2] + e[3])

    def tiles(lo, hi, js, extra=None):
        def step(n, _):
            k = near(n)
            for j in js:
                tile(k, j)
            if extra is not None:
                extra(k)
            return 0

        lax.fori_loop(lo, hi, step, 0)

    def turn(k):
        row0 = pl.multiple_of(k * R2, R2)
        img_t[:, pl.ds(row0, R2)] = img_all[pl.ds(row0, R2), :].T

    def finish_rows(k):
        for r in range(2):
            rows = pl.ds(pl.multiple_of(k * R2 + r * B, B), B)
            top = jnp.maximum(
                jnp.maximum(rm_ref[0, rows, :], rm_ref[1, rows, :]), jnp.maximum(rm_ref[2, rows, :], rm_ref[3, rows, :])
            )
            total = rl_ref[0, rows, :] * jnp.exp2(rm_ref[0, rows, :] - top)
            for j in range(1, 4):
                total = total + rl_ref[j, rows, :] * jnp.exp2(rm_ref[j, rows, :] - top)
            mt, lt = top.T, total.T
            top = jnp.max(mt, 0, keepdims=True)
            total = jnp.sum(lt * jnp.exp2(mt - top), 0, keepdims=True)
            msg_r[pl.ds(r * NZ + k, 1), :] = top + jnp.log(total) * LOG2E

    for i in (1, 3, 2):
        txt_first(i).wait_recv()
    for j in (1, 3, 2):
        txt_second(j).start()
    for k in (1, 7):
        img_copy(k).wait_recv()
        sib_copy(k).start()
    sib_copy(0).wait_recv()
    tiles(0, 1, (0,), turn)
    for k in (2, 6):
        img_copy(k).wait_recv()
    img_forward(3).start()
    img_forward(5).start()
    img_forward(4, 0).start()
    img_forward(4, 1).start()
    for k in (2, 6):
        sib_copy(k).start()
    for k in (1, 7, 2, 6):
        sib_copy(k).wait_recv()
    tiles(1, 5, (0,), turn)
    txt_second(1).wait_recv()
    tiles(0, 5, (1,))
    img_forward(3).wait_recv()
    img_forward(5).wait_recv()
    sib_copy(3).start()
    sib_copy(5).start()
    txt_second(3).wait_recv()
    tiles(0, 5, (3,))
    img_forward(4, 0).wait_recv()
    img_forward(4, 1).wait_recv()
    sib_copy(4).start()
    for k in (3, 5):
        sib_copy(k).wait_recv()
    tiles(5, 7, (0, 1, 3), turn)
    sib_copy(4).wait_recv()
    tiles(7, 8, (0, 1, 3), turn)
    txt_second(2).wait_recv()
    tiles(0, 8, (2,), finish_rows)

    for i in (1, 3, 2):
        txt_first(i).wait_send()
    for j in (1, 3, 2):
        txt_second(j).wait_send()
    for k in (1, 2, 6, 7):
        img_copy(k).wait_send()
    for k, h in ((3, None), (5, None), (4, 0), (4, 1)):
        img_forward(k, h).wait_send()
    for k in range(NZ):
        sib_copy(k).wait_send()

    for cc in range(COLS // 128):
        lanes = slice(cc * 128, (cc + 1) * 128)
        mt = cm_ref[:, :, lanes].reshape(NZ * 8, 128)
        lt = cl_ref[:, :, lanes].reshape(NZ * 8, 128)
        top = jnp.max(mt, 0, keepdims=True)
        total = jnp.sum(lt * jnp.exp2(mt - top), 0, keepdims=True)
        msg_c[cc : cc + 1, :] = top + jnp.log(total) * LOG2E

    def row_msg(d, r):
        q = d * 2 + r
        return rcopy(msg_r, got_r.at[q], mr_s.at[q], mr_r.at[q], dev(0, 0, d, r))

    def col_msg(i, j):
        q = j * 4 + i
        return rcopy(msg_c, got_c.at[q], mc_s.at[q], mc_r.at[q], dev_ab(i, j))

    for d, r in row_peers:
        row_msg(d, r).start()
    for i, j in col_peers:
        col_msg(i, j).start()

    def combine(parts):
        top = parts[0]
        for p in parts[1:]:
            top = jnp.maximum(top, p)
        total = jnp.exp2(parts[0] - top)
        for p in parts[1:]:
            total = total + jnp.exp2(p - top)
        return top + jnp.log(total) * LOG2E

    for d, r in row_peers:
        row_msg(d, r).wait()
    halves = ([], [])
    diag = msg_r[16:24, :]
    for d in range(NZ):
        for r in range(2):
            ref = msg_r if (d, r) == (0, 0) else got_r.at[d * 2 + r]
            if (d, r) != (0, 0):
                diag = diag + ref[16:24, :]
            for rs in range(2):
                v = ref[rs * 8 : rs * 8 + 8, :]
                halves[rs ^ r].append(pltpu.roll(v, d, 0) if d else v)
    lr = [combine(h) for h in halves]

    for i, j in col_peers:
        col_msg(i, j).wait()
    jj = lax.broadcasted_iota(jnp.int32, (NX * NY, 128), 0) % NY
    parts = []
    for a in range(NX):
        for b in range(NY):
            v = msg_c[...] if (a, b) == (0, 0) else got_c[a * NY + b]
            s1, s2 = (4 * a + b) % 16, (4 * a + b + 12) % 16
            if b == 0:
                v = pltpu.roll(v, s1, 0) if s1 else v
            else:
                v = jnp.where(jj >= b, pltpu.roll(v, s1, 0), pltpu.roll(v, s2, 0) if s2 else v)
            parts.append(v)
    lc = combine(parts)
    lc_ref[...] = lc + 1.0

    out_a[...] = (lr[0] + lr[1]) * LN2 - (2.0 * factor) * diag
    out_b[...] = (lc[0:8] + lc[8:16]) * LN2

    def a_msg(i, j):
        q = j * 4 + i
        return rcopy(out_a, got_a.at[q], la_s.at[q], la_r.at[q], dev_ab(i, j))

    def b_msg(d, r):
        q = d * 2 + r
        return rcopy(out_b, got_b.at[q], lb_s.at[q], lb_r.at[q], dev(0, 0, d, r))

    for i, j in col_peers:
        a_msg(i, j).start()
    for d, r in row_peers:
        b_msg(d, r).start()

    for k in range(NZ):
        for r in range(2):
            lrb_ref[k * R2 + r * B : k * R2 + (r + 1) * B, :] = (
                jnp.broadcast_to(lr[r][k : k + 1, :], (B, 128)) + 1.0
            ).T

    def order(n):
        return jnp.where(n % 2 == 0, NZ // 2 - n // 2, (NZ // 2 + (n + 1) // 2) % NZ)

    def sib_part(k):
        return rcopy(sib_out.at[k], sib_in.at[k], sb_s.at[k], sb_r.at[k], dev(0, 0, 0, 1))

    def far_part(k):
        return rcopy(far_out.at[k], far_in.at[k], fo_s.at[k], fo_r.at[k], dev(0, 0, -k, 0))

    def pass_on(k):
        sib_part(k).wait_recv()
        far_out[k] = (keep_i[k] + sib_in[k]).astype(BF16)
        far_part(k).start()

    def second_step(n, _):
        k = order(n)
        row0 = pl.multiple_of(k * R2, R2)
        rows = pl.ds(row0, R2)
        for cc in range(COLS // 128):
            lanes = slice(cc * 128, (cc + 1) * 128)
            s = s_ref[rows, lanes]
            w = jnp.exp2(s - lrb_ref[rows, :]) + jnp.exp2(s - lc_ref[cc : cc + 1, :])
            w_ref[rows, lanes] = w.astype(BF16)
        part = jnp.dot(w_ref[rows, :], txt_all[...], preferred_element_type=F32)
        keep_i[k] = part[0:B]
        sib_out[k] = part[B:R2]
        sib_part(k).start()

        @pl.when(n > 0)
        def _():
            pass_on(order(n - 1))

        return 0

    lax.fori_loop(0, NZ, second_step, 0)

    def txt_part(q):
        return rcopy(t_out.at[q], t_in.at[q], to_s.at[q], to_r.at[q], dev_ab(-(q % 4), -(q // 4)))

    def third(cc):
        return jnp.dot(img_t[...], w_ref[:, pl.ds(pl.multiple_of(cc * 256, 256), 256)], preferred_element_type=F32)

    def third_step(n, _):
        cc = COLS // 256 - 1 - n
        part = third(cc)
        for h in range(2):
            t_out[2 * cc + h] = part[:, h * 128 : (h + 1) * 128].astype(BF16)
            txt_part(2 * cc + h).start()
        return 0

    lax.fori_loop(0, COLS // 256 - 1, third_step, 0)
    part = third(0)
    keep_t[...] = part[:, 0:128]
    t_out[1] = part[:, 128:256].astype(BF16)
    txt_part(1).start()

    sib_part(0).wait_recv()
    total = keep_i[0] + sib_in[0]
    for k in range(1, NZ):
        far_part(k).wait_recv()
        total = total + far_in[k].astype(F32)
    gi_ref[...] = factor * (total - txt_ref[...].astype(F32))

    for i, j in col_peers:
        a_msg(i, j).wait()
    for d, r in row_peers:
        b_msg(d, r).wait()
    share = out_a[...] + out_b[...]
    for q in range(1, 16):
        share = share + got_a[q] + got_b[q]
    loss_ref[0] = jnp.sum(share) / (2.0 * 256 * B)

    total = keep_t[...]
    for q in range(1, 16):
        txt_part(q).wait_recv()
        total = total + t_in[q].astype(F32)
    gt_ref[...] = factor * (total.T - img_ref[...].astype(F32))

    for k in range(NZ):
        sib_part(k).wait_send()
    for k in range(1, NZ):
        far_part(k).wait_send()
    for q in range(1, 16):
        txt_part(q).wait_send()


def local(images, texts, logit_scale):
    dma = pltpu.SemaphoreType.DMA
    vm = pltpu.VMEM
    return pl.pallas_call(
        kernel,
        out_shape=(
            jax.ShapeDtypeStruct((1,), F32),
            jax.ShapeDtypeStruct((B, E), F32),
            jax.ShapeDtypeStruct((B, E), F32),
        ),
        in_specs=[
            pl.BlockSpec(memory_space=pltpu.SMEM),
            pl.BlockSpec(memory_space=vm),
            pl.BlockSpec(memory_space=vm),
        ],
        out_specs=(
            pl.BlockSpec(memory_space=pltpu.SMEM),
            pl.BlockSpec(memory_space=vm),
            pl.BlockSpec(memory_space=vm),
        ),
        scratch_shapes=[
            vm((ROWS, E), BF16), vm((COLS, E), BF16), vm((E, ROWS), BF16),
            vm((ROWS, COLS), F32), vm((ROWS, COLS), BF16),
            vm((4, ROWS, 128), F32), vm((4, ROWS, 128), F32), vm((NZ, 8, COLS), F32), vm((NZ, 8, COLS), F32),
            vm((ROWS, 128), F32), vm((16, 128), F32),
            vm((24, 128), F32), vm((16, 128), F32), vm((16, 24, 128), F32), vm((16, 16, 128), F32),
            vm((8, 128), F32), vm((8, 128), F32), vm((16, 8, 128), F32), vm((16, 8, 128), F32),
            vm((NZ, B, E), F32), vm((NZ, B, E), F32), vm((NZ, B, E), F32),
            vm((NZ, B, E), BF16), vm((NZ, B, E), BF16),
            vm((E, B), F32), vm((16, E, B), BF16), vm((16, E, B), BF16),
            dma((9,)), dma((9,)), dma((NZ,)), dma((NZ,)), dma((16,)), dma((16,)),
            dma((16,)), dma((16,)), dma((16,)), dma((16,)),
            dma((16,)), dma((16,)), dma((16,)), dma((16,)),
            dma((NZ,)), dma((NZ,)), dma((NZ,)), dma((NZ,)), dma((16,)), dma((16,)),
        ],
        compiler_params=pltpu.CompilerParams(
            collective_id=0, has_side_effects=True, vmem_limit_bytes=56 * 1024 * 1024
        ),
        cost_estimate=pl.CostEstimate(
            flops=6 * ROWS * COLS * E, bytes_accessed=8 * B * E, transcendentals=4 * ROWS * COLS
        ),
    )(logit_scale, images, texts)


def solution(mesh):
    spec = P(("outer", "inner"), None)
    return jax.shard_map(
        local, mesh=mesh, in_specs=(spec, spec, P()), out_specs=(P(), spec, spec), check_vma=False
    )
```

```python
import math

import jax
import jax.numpy as jnp
from jax import lax
from jax.experimental import pallas as pl
from jax.experimental.pallas import tpu as pltpu
from jax.sharding import PartitionSpec as P

MESH = pl.DeviceIdType.MESH
F32 = jnp.float32
BF16 = jnp.bfloat16
B = 128
E = 384
NX, NY, NZ = 4, 4, 8
ROWS = NZ * 2 * B
COLS = NX * NY * B
R2 = 2 * B
QC = 4 * B
LOG2E = math.log2(math.e)
LN2 = math.log(2.0)


def nt(a, b):
    return lax.dot_general(a, b, (((1,), (1,)), ((), ())), preferred_element_type=F32)


def kernel(
    scale_ref, img_ref, txt_ref, loss_ref, gi_ref, gt_ref,
    img_all, txt_all, img_t, s_ref, w_ref,
    rm_ref, rl_ref, cm_ref, cl_ref, lrb_ref, lc_ref,
    msg_r, msg_c, got_r, got_c, out_a, out_b, got_a, got_b,
    keep_i, sib_out, sib_in, far_out, far_in, mid_in, keep_t, t_out, t_in, u_out, u_in,
    is_s, is_r, fs_s, fs_r, ts_s, ts_r, mr_s, mr_r, mc_s, mc_r,
    la_s, la_r, lb_s, lb_r, sb_s, sb_r, fo_s, fo_r, to_s, to_r,
):
    outer, inner = lax.axis_index("outer"), lax.axis_index("inner")
    c = outer % 2
    x = (outer // 2) % NX
    y = (outer // (2 * NX)) * 2 + inner // NZ
    z = inner % NZ
    factor = scale_ref[0]
    f2 = factor * LOG2E

    def dev(dx, dy, dz, dc):
        xx, yy, zz = (x + dx + NX) % NX, (y + dy + NY) % NY, (z + dz + NZ) % NZ
        cc = (c + dc) % 2
        return ((yy // 2) * (2 * NX) + xx * 2 + cc, (yy % 2) * NZ + zz)

    def dev_ab(da, db):
        return dev(jnp.where(c == 0, da, db), jnp.where(c == 0, db, da), 0, 0)

    def rcopy(src, dst, ss, rs, to):
        return pltpu.make_async_remote_copy(
            src_ref=src, dst_ref=dst, send_sem=ss, recv_sem=rs, device_id=to, device_id_type=MESH
        )

    barrier = pltpu.get_barrier_semaphore()
    row_peers = [(d, r) for d in range(NZ) for r in range(2) if (d, r) != (0, 0)]
    col_peers = [(i, j) for i in range(NX) for j in range(NY) if (i, j) != (0, 0)]
    for d, r in row_peers:
        pl.semaphore_signal(barrier, inc=1, device_id=dev(0, 0, d, r), device_id_type=MESH)
    for i, j in col_peers:
        pl.semaphore_signal(barrier, inc=1, device_id=dev_ab(i, j), device_id_type=MESH)
    pl.semaphore_wait(barrier, len(row_peers) + len(col_peers))

    def img_rows(k, h=None):
        return img_all.at[pl.ds(k * R2, B)] if h is None else img_all.at[pl.ds(k * R2 + h * 64, 64)]

    def img_copy(k):
        return rcopy(img_ref, img_rows(k), is_s.at[k], is_r.at[k], dev(0, 0, k, 0))

    def img_forward(k, h=None):
        if k == 3:
            return rcopy(img_rows(2), img_rows(3), is_s.at[3], is_r.at[3], dev(0, 0, 1, 0))
        if k == 5:
            return rcopy(img_rows(6), img_rows(5), is_s.at[5], is_r.at[5], dev(0, 0, -1, 0))
        if h == 0:
            return rcopy(img_rows(2, 0), img_rows(4, 0), is_s.at[4], is_r.at[4], dev(0, 0, 2, 0))
        return rcopy(img_rows(6, 1), img_rows(4, 1), is_s.at[8], is_r.at[8], dev(0, 0, -2, 0))

    def sib_copy(k):
        return rcopy(img_rows(k), img_all.at[pl.ds(k * R2 + B, B)], fs_s.at[k], fs_r.at[k], dev(0, 0, 0, 1))

    def txt_first(i):
        return rcopy(txt_ref, txt_all.at[pl.ds(i * B, B)], ts_s.at[i], ts_r.at[i], dev_ab(i, 0))

    def txt_second(j):
        return rcopy(
            txt_all.at[pl.ds(0, QC)], txt_all.at[pl.ds(j * QC, QC)], ts_s.at[3 + j], ts_r.at[3 + j], dev_ab(0, j)
        )

    img_all[0:B, :] = img_ref[...]
    txt_all[0:B, :] = txt_ref[...]
    for i in (1, 3, 2):
        txt_first(i).start()
    for k in (2, 6, 1, 7):
        img_copy(k).start()
    sib_copy(0).start()

    prod = img_ref[...].astype(F32) * txt_ref[...].astype(F32)
    prod = prod[:, 0:128] + prod[:, 128:256] + prod[:, 256:384]
    msg_r[16:24, :] = jnp.sum(prod.reshape(B // 8, 8, 128), 0)

    def near(n):
        return jnp.where(n % 2 == 1, (n + 1) // 2, (NZ - n // 2) % NZ)

    def tile(k, j):
        row0 = pl.multiple_of(k * R2, R2)
        block = img_all[pl.ds(row0, R2), :]
        for cc in range(j * 2, j * 2 + 2):
            s = nt(block, txt_all[cc * 256 : (cc + 1) * 256, :]) * f2
            s_ref[pl.ds(row0, R2), cc * 256 : (cc + 1) * 256] = s
        for cc in range(j * 4, j * 4 + 4):
            lanes = slice(cc * 128, (cc + 1) * 128)
            slab = s_ref[pl.ds(row0, R2), lanes].reshape(R2 // 8, 8, 128)
            top = jnp.max(slab, 0)
            cm_ref[k, :, lanes] = top
            cl_ref[k, :, lanes] = jnp.sum(jnp.exp2(slab - top[None]), 0)
        for rr in range(R2 // 32):
            rows = pl.ds(row0 + rr * 32, 32)
            parts = [s_ref[rows, cc * 128 : (cc + 1) * 128] for cc in range(j * 4, j * 4 + 4)]
            top = jnp.maximum(jnp.maximum(parts[0], parts[1]), jnp.maximum(parts[2], parts[3]))
            e = [jnp.exp2(p - top) for p in parts]
            rm_ref[j, rows, :] = top
            rl_ref[j, rows, :] = (e[0] + e[1]) + (e[2] + e[3])

    def tiles(lo, hi, js, extra=None):
        def step(n, _):
            k = near(n)
            for j in js:
                tile(k, j)
            if extra is not None:
                extra(k)
            return 0

        lax.fori_loop(lo, hi, step, 0)

    def turn(k):
        row0 = pl.multiple_of(k * R2, R2)
        img_t[:, pl.ds(row0, R2)] = img_all[pl.ds(row0, R2), :].T

    def finish_rows(k):
        for r in range(2):
            rows = pl.ds(pl.multiple_of(k * R2 + r * B, B), B)
            top = jnp.maximum(
                jnp.maximum(rm_ref[0, rows, :], rm_ref[1, rows, :]), jnp.maximum(rm_ref[2, rows, :], rm_ref[3, rows, :])
            )
            total = rl_ref[0, rows, :] * jnp.exp2(rm_ref[0, rows, :] - top)
            for j in range(1, 4):
                total = total + rl_ref[j, rows, :] * jnp.exp2(rm_ref[j, rows, :] - top)
            mt, lt = top.T, total.T
            top = jnp.max(mt, 0, keepdims=True)
            total = jnp.sum(lt * jnp.exp2(mt - top), 0, keepdims=True)
            msg_r[pl.ds(r * NZ + k, 1), :] = top + jnp.log(total) * LOG2E

    for i in (1, 3, 2):
        txt_first(i).wait_recv()
    for j in (1, 3, 2):
        txt_second(j).start()
    for k in (1, 7):
        img_copy(k).wait_recv()
        sib_copy(k).start()
    sib_copy(0).wait_recv()
    tiles(0, 1, (0,), turn)
    for k in (2, 6):
        img_copy(k).wait_recv()
    img_forward(3).start()
    img_forward(5).start()
    img_forward(4, 0).start()
    img_forward(4, 1).start()
    for k in (2, 6):
        sib_copy(k).start()
    for k in (1, 7, 2, 6):
        sib_copy(k).wait_recv()
    tiles(1, 5, (0,), turn)
    txt_second(1).wait_recv()
    tiles(0, 5, (1,))
    img_forward(3).wait_recv()
    img_forward(5).wait_recv()
    sib_copy(3).start()
    sib_copy(5).start()
    txt_second(3).wait_recv()
    tiles(0, 5, (3,))
    img_forward(4, 0).wait_recv()
    img_forward(4, 1).wait_recv()
    sib_copy(4).start()
    for k in (3, 5):
        sib_copy(k).wait_recv()
    tiles(5, 7, (0, 1, 3), turn)
    sib_copy(4).wait_recv()
    tiles(7, 8, (0, 1, 3), turn)
    txt_second(2).wait_recv()
    tiles(0, 8, (2,), finish_rows)

    for i in (1, 3, 2):
        txt_first(i).wait_send()
    for j in (1, 3, 2):
        txt_second(j).wait_send()
    for k in (1, 2, 6, 7):
        img_copy(k).wait_send()
    for k, h in ((3, None), (5, None), (4, 0), (4, 1)):
        img_forward(k, h).wait_send()
    for k in range(NZ):
        sib_copy(k).wait_send()

    for cc in range(COLS // 128):
        lanes = slice(cc * 128, (cc + 1) * 128)
        mt = cm_ref[:, :, lanes].reshape(NZ * 8, 128)
        lt = cl_ref[:, :, lanes].reshape(NZ * 8, 128)
        top = jnp.max(mt, 0, keepdims=True)
        total = jnp.sum(lt * jnp.exp2(mt - top), 0, keepdims=True)
        msg_c[cc : cc + 1, :] = top + jnp.log(total) * LOG2E

    def row_msg(d, r):
        q = d * 2 + r
        return rcopy(msg_r, got_r.at[q], mr_s.at[q], mr_r.at[q], dev(0, 0, d, r))

    def col_msg(i, j):
        q = j * 4 + i
        return rcopy(msg_c, got_c.at[q], mc_s.at[q], mc_r.at[q], dev_ab(i, j))

    for d, r in row_peers:
        row_msg(d, r).start()
    for i, j in col_peers:
        col_msg(i, j).start()

    def combine(parts):
        top = parts[0]
        for p in parts[1:]:
            top = jnp.maximum(top, p)
        total = jnp.exp2(parts[0] - top)
        for p in parts[1:]:
            total = total + jnp.exp2(p - top)
        return top + jnp.log(total) * LOG2E

    for d, r in row_peers:
        row_msg(d, r).wait()
    halves = ([], [])
    diag = msg_r[16:24, :]
    for d in range(NZ):
        for r in range(2):
            ref = msg_r if (d, r) == (0, 0) else got_r.at[d * 2 + r]
            if (d, r) != (0, 0):
                diag = diag + ref[16:24, :]
            for rs in range(2):
                v = ref[rs * 8 : rs * 8 + 8, :]
                halves[rs ^ r].append(pltpu.roll(v, d, 0) if d else v)
    lr = [combine(h) for h in halves]

    for i, j in col_peers:
        col_msg(i, j).wait()
    jj = lax.broadcasted_iota(jnp.int32, (NX * NY, 128), 0) % NY
    parts = []
    for a in range(NX):
        for b in range(NY):
            v = msg_c[...] if (a, b) == (0, 0) else got_c[a * NY + b]
            s1, s2 = (4 * a + b) % 16, (4 * a + b + 12) % 16
            if b == 0:
                v = pltpu.roll(v, s1, 0) if s1 else v
            else:
                v = jnp.where(jj >= b, pltpu.roll(v, s1, 0), pltpu.roll(v, s2, 0) if s2 else v)
            parts.append(v)
    lc = combine(parts)
    lc_ref[...] = lc + 1.0

    out_a[...] = (lr[0] + lr[1]) * LN2 - (2.0 * factor) * diag
    out_b[...] = (lc[0:8] + lc[8:16]) * LN2

    def a_msg(i, j):
        q = j * 4 + i
        return rcopy(out_a, got_a.at[q], la_s.at[q], la_r.at[q], dev_ab(i, j))

    def b_msg(d, r):
        q = d * 2 + r
        return rcopy(out_b, got_b.at[q], lb_s.at[q], lb_r.at[q], dev(0, 0, d, r))

    for i, j in col_peers:
        a_msg(i, j).start()
    for d, r in row_peers:
        b_msg(d, r).start()

    for k in range(NZ):
        for r in range(2):
            lrb_ref[k * R2 + r * B : k * R2 + (r + 1) * B, :] = (
                jnp.broadcast_to(lr[r][k : k + 1, :], (B, 128)) + 1.0
            ).T

    def sib_part(k):
        return rcopy(sib_out.at[k], sib_in.at[k], sb_s.at[k], sb_r.at[k], dev(0, 0, 0, 1))

    def far_part(k):
        if k == 3:
            return rcopy(far_out.at[3], mid_in.at[0], fo_s.at[3], fo_r.at[3], dev(0, 0, -1, 0))
        if k == 5:
            return rcopy(far_out.at[5], mid_in.at[1], fo_s.at[5], fo_r.at[5], dev(0, 0, 1, 0))
        if k == 4:
            rows = pl.ds(0, 64)
            return rcopy(far_out.at[4, rows], mid_in.at[2, rows], fo_s.at[4], fo_r.at[4], dev(0, 0, -2, 0))
        if k == 8:
            rows = pl.ds(64, 64)
            return rcopy(far_out.at[4, rows], mid_in.at[2, rows], fo_s.at[8], fo_r.at[8], dev(0, 0, 2, 0))
        return rcopy(far_out.at[k], far_in.at[k], fo_s.at[k], fo_r.at[k], dev(0, 0, -k, 0))

    def pass_on(k):
        sib_part(k).wait_recv()
        total = keep_i[k] + sib_in[k]
        if k in (2, 6):
            half = 0 if k == 2 else 1
            far_part(3 if k == 2 else 5).wait_recv()
            far_part(4 if k == 2 else 8).wait_recv()
            total = total + mid_in[half].astype(F32)
            h = slice(half * 64, half * 64 + 64)
            far_out[k] = total.astype(BF16)
            far_out[k, h, :] = (total[h] + mid_in[2, h, :].astype(F32)).astype(BF16)
        else:
            far_out[k] = total.astype(BF16)
        far_part(k).start()
        if k == 4:
            far_part(8).start()

    def weigh(k, js):
        row0 = pl.multiple_of(k * R2, R2)
        rows = pl.ds(row0, R2)
        for j in js:
            for cc in range(j * 4, j * 4 + 4):
                lanes = slice(cc * 128, (cc + 1) * 128)
                s = s_ref[rows, lanes]
                w = jnp.exp2(s - lrb_ref[rows, :]) + jnp.exp2(s - lc_ref[cc : cc + 1, :])
                w_ref[rows, lanes] = w.astype(BF16)

    def txt_part(j):
        return rcopy(t_out.at[j], t_in.at[j], to_s.at[j], to_r.at[j], dev_ab(0, -j))

    def txt_part2(i):
        return rcopy(u_out.at[i], u_in.at[i], to_s.at[4 + i], to_r.at[4 + i], dev_ab(-i, 0))

    def third(j):
        return jnp.dot(img_t[...], w_ref[:, j * QC : (j + 1) * QC], preferred_element_type=F32)

    def send_quarter(j):
        t_out[j] = third(j).astype(BF16)
        txt_part(j).start()

    for j in (2, 1):
        lax.fori_loop(0, NZ, lambda k, t, j=j: (weigh(k, (j,)), t)[1], 0)
        send_quarter(j)

    ks = (4, 3, 5, 1, 7, 2, 6, 0)
    for n, k in enumerate(ks):
        weigh(k, (0, 3))
        part = jnp.dot(w_ref[k * R2 : (k + 1) * R2, :], txt_all[...], preferred_element_type=F32)
        keep_i[k] = part[0:B]
        sib_out[k] = part[B:R2]
        sib_part(k).start()
        if 1 <= n <= 5:
            pass_on(ks[n - 1])
    send_quarter(3)
    pass_on(2)
    pass_on(6)
    keep_t[...] = third(0)

    for i, j in col_peers:
        a_msg(i, j).wait()
    for d, r in row_peers:
        b_msg(d, r).wait()
    share = out_a[...] + out_b[...]
    for q in range(1, 16):
        share = share + got_a[q] + got_b[q]
    loss_ref[0] = jnp.sum(share) / (2.0 * 256 * B)

    for j in (2, 1, 3):
        txt_part(j).wait_recv()
    for i in (2, 1, 3, 0):
        h = slice(i * B, (i + 1) * B)
        total = keep_t[:, h] + t_in[1, :, h].astype(F32) + t_in[2, :, h].astype(F32) + t_in[3, :, h].astype(F32)
        if i:
            u_out[i] = total.astype(BF16)
            txt_part2(i).start()
        else:
            own_t = total

    sib_part(0).wait_recv()
    total = keep_i[0] + sib_in[0]
    for k in (1, 7, 2, 6):
        far_part(k).wait_recv()
        total = total + far_in[k].astype(F32)
    gi_ref[...] = factor * (total - txt_ref[...].astype(F32))

    for i in (1, 3, 2):
        txt_part2(i).wait_recv()
        own_t = own_t + u_in[i].astype(F32)
    gt_ref[...] = factor * (own_t.T - img_ref[...].astype(F32))

    for k in range(NZ):
        sib_part(k).wait_send()
    for k in range(1, NZ + 1):
        far_part(k).wait_send()
    for j in range(1, 4):
        txt_part(j).wait_send()
        txt_part2(j).wait_send()


def local(images, texts, logit_scale):
    dma = pltpu.SemaphoreType.DMA
    vm = pltpu.VMEM
    return pl.pallas_call(
        kernel,
        out_shape=(
            jax.ShapeDtypeStruct((1,), F32),
            jax.ShapeDtypeStruct((B, E), F32),
            jax.ShapeDtypeStruct((B, E), F32),
        ),
        in_specs=[
            pl.BlockSpec(memory_space=pltpu.SMEM),
            pl.BlockSpec(memory_space=vm),
            pl.BlockSpec(memory_space=vm),
        ],
        out_specs=(
            pl.BlockSpec(memory_space=pltpu.SMEM),
            pl.BlockSpec(memory_space=vm),
            pl.BlockSpec(memory_space=vm),
        ),
        scratch_shapes=[
            vm((ROWS, E), BF16), vm((COLS, E), BF16), vm((E, ROWS), BF16),
            vm((ROWS, COLS), F32), vm((ROWS, COLS), BF16),
            vm((4, ROWS, 128), F32), vm((4, ROWS, 128), F32), vm((NZ, 8, COLS), F32), vm((NZ, 8, COLS), F32),
            vm((ROWS, 128), F32), vm((16, 128), F32),
            vm((24, 128), F32), vm((16, 128), F32), vm((16, 24, 128), F32), vm((16, 16, 128), F32),
            vm((8, 128), F32), vm((8, 128), F32), vm((16, 8, 128), F32), vm((16, 8, 128), F32),
            vm((NZ, B, E), F32), vm((NZ, B, E), F32), vm((NZ, B, E), F32),
            vm((NZ, B, E), BF16), vm((NZ, B, E), BF16), vm((3, B, E), BF16),
            vm((E, QC), F32), vm((4, E, QC), BF16), vm((4, E, QC), BF16), vm((4, E, B), BF16), vm((4, E, B), BF16),
            dma((9,)), dma((9,)), dma((NZ,)), dma((NZ,)), dma((16,)), dma((16,)),
            dma((16,)), dma((16,)), dma((16,)), dma((16,)),
            dma((16,)), dma((16,)), dma((16,)), dma((16,)),
            dma((NZ,)), dma((NZ,)), dma((9,)), dma((9,)), dma((8,)), dma((8,)),
        ],
        compiler_params=pltpu.CompilerParams(
            collective_id=0, has_side_effects=True, vmem_limit_bytes=56 * 1024 * 1024
        ),
        cost_estimate=pl.CostEstimate(
            flops=6 * ROWS * COLS * E, bytes_accessed=8 * B * E, transcendentals=4 * ROWS * COLS
        ),
    )(logit_scale, images, texts)


def solution(mesh):
    spec = P(("outer", "inner"), None)
    return jax.shard_map(
        local, mesh=mesh, in_specs=(spec, spec, P()), out_specs=(P(), spec, spec), check_vma=False
    )
```

```python
import math

import jax
import jax.numpy as jnp
from jax import lax
from jax.experimental import pallas as pl
from jax.experimental.pallas import tpu as pltpu
from jax.sharding import PartitionSpec as P

MESH = pl.DeviceIdType.MESH
F32 = jnp.float32
BF16 = jnp.bfloat16
B = 128
E = 384
NX, NY, NZ = 4, 4, 8
ROWS = NZ * 2 * B
COLS = NX * NY * B
R2 = 2 * B
QC = 4 * B
LOG2E = math.log2(math.e)
LN2 = math.log(2.0)


def nt(a, b):
    return lax.dot_general(a, b, (((1,), (1,)), ((), ())), preferred_element_type=F32)


def kernel(
    scale_ref, img_ref, txt_ref, loss_ref, gi_ref, gt_ref,
    img_all, txt_all, img_t, s_ref, w_ref,
    rm_ref, rl_ref, cm_ref, cl_ref, lrb_ref, lc_ref,
    msg_r, msg_c, got_r, got_c, out_a, out_b, got_a, got_b,
    keep_i, sib_out, sib_in, far_out, far_in, mid_in, keep_t, t_out, t_in, u_out, u_in,
    is_s, is_r, fs_s, fs_r, ts_s, ts_r, mr_s, mr_r, mc_s, mc_r,
    la_s, la_r, lb_s, lb_r, sb_s, sb_r, fo_s, fo_r, to_s, uo_s, to_r,
):
    outer, inner = lax.axis_index("outer"), lax.axis_index("inner")
    c = outer % 2
    x = (outer // 2) % NX
    y = (outer // (2 * NX)) * 2 + inner // NZ
    z = inner % NZ
    factor = scale_ref[0]
    f2 = factor * LOG2E

    def dev(dx, dy, dz, dc):
        xx, yy, zz = (x + dx + NX) % NX, (y + dy + NY) % NY, (z + dz + NZ) % NZ
        cc = (c + dc) % 2
        return ((yy // 2) * (2 * NX) + xx * 2 + cc, (yy % 2) * NZ + zz)

    def dev_ab(da, db):
        return dev(jnp.where(c == 0, da, db), jnp.where(c == 0, db, da), 0, 0)

    def rcopy(src, dst, ss, rs, to):
        return pltpu.make_async_remote_copy(
            src_ref=src, dst_ref=dst, send_sem=ss, recv_sem=rs, device_id=to, device_id_type=MESH
        )

    def drain(ref, sem):
        pltpu.make_async_copy(ref, ref, sem).wait()

    barrier = pltpu.get_barrier_semaphore()
    row_peers = [(d, r) for d in range(NZ) for r in range(2) if (d, r) != (0, 0)]
    col_peers = [(i, j) for i in range(NX) for j in range(NY) if (i, j) != (0, 0)]
    for d, r in row_peers:
        pl.semaphore_signal(barrier, inc=1, device_id=dev(0, 0, d, r), device_id_type=MESH)
    for i, j in col_peers:
        pl.semaphore_signal(barrier, inc=1, device_id=dev_ab(i, j), device_id_type=MESH)
    pl.semaphore_wait(barrier, len(row_peers) + len(col_peers))

    def img_rows(k, h=None):
        return img_all.at[pl.ds(k * R2, B)] if h is None else img_all.at[pl.ds(k * R2 + h * 64, 64)]

    def img_copy(k):
        return rcopy(img_ref, img_rows(k), is_s, is_r.at[k], dev(0, 0, k, 0))

    def img_forward(k, h=None):
        if k == 3:
            return rcopy(img_rows(2), img_rows(3), is_s, is_r.at[3], dev(0, 0, 1, 0))
        if k == 5:
            return rcopy(img_rows(6), img_rows(5), is_s, is_r.at[5], dev(0, 0, -1, 0))
        if h == 0:
            return rcopy(img_rows(2, 0), img_rows(4, 0), is_s, is_r.at[4], dev(0, 0, 2, 0))
        return rcopy(img_rows(6, 1), img_rows(4, 1), is_s, is_r.at[8], dev(0, 0, -2, 0))

    def sib_copy(k):
        return rcopy(img_rows(k), img_all.at[pl.ds(k * R2 + B, B)], fs_s, fs_r.at[k], dev(0, 0, 0, 1))

    def txt_first(i):
        return rcopy(txt_ref, txt_all.at[pl.ds(i * B, B)], ts_s, ts_r.at[i], dev_ab(i, 0))

    def txt_second(i, j):
        return rcopy(
            txt_all.at[pl.ds(i * B, B)], txt_all.at[pl.ds((j * 4 + i) * B, B)], ts_s, ts_r.at[3 + j], dev_ab(0, j)
        )

    def txt_quarter(j):
        drain(txt_all.at[pl.ds(j * QC, QC)], ts_r.at[3 + j])

    img_all[0:B, :] = img_ref[...]
    txt_all[0:B, :] = txt_ref[...]
    for i in (1, 3, 2):
        txt_first(i).start()
    for k in (2, 6, 1, 7):
        img_copy(k).start()
    for j in (1, 3, 2):
        txt_second(0, j).start()
    sib_copy(0).start()

    prod = img_ref[...].astype(F32) * txt_ref[...].astype(F32)
    prod = prod[:, 0:128] + prod[:, 128:256] + prod[:, 256:384]
    msg_r[16:24, :] = jnp.sum(prod.reshape(B // 8, 8, 128), 0)

    def tile(k, j):
        row0 = k * R2
        block = img_all[row0 : row0 + R2, :]
        for cc in range(j * 2, j * 2 + 2):
            s = nt(block, txt_all[cc * 256 : (cc + 1) * 256, :]) * f2
            s_ref[row0 : row0 + R2, cc * 256 : (cc + 1) * 256] = s
        for cc in range(j * 4, j * 4 + 4):
            lanes = slice(cc * 128, (cc + 1) * 128)
            slab = s_ref[row0 : row0 + R2, lanes].reshape(R2 // 8, 8, 128)
            top = jnp.max(slab, 0)
            cm_ref[k, :, lanes] = top
            cl_ref[k, :, lanes] = jnp.sum(jnp.exp2(slab - top[None]), 0)
        for rr in range(R2 // 32):
            rows = slice(row0 + rr * 32, row0 + rr * 32 + 32)
            parts = [s_ref[rows, cc * 128 : (cc + 1) * 128] for cc in range(j * 4, j * 4 + 4)]
            top = jnp.maximum(jnp.maximum(parts[0], parts[1]), jnp.maximum(parts[2], parts[3]))
            e = [jnp.exp2(p - top) for p in parts]
            rm_ref[j, rows, :] = top
            rl_ref[j, rows, :] = (e[0] + e[1]) + (e[2] + e[3])

    def tiles(ks, js):
        for j in js:
            for k in ks:
                tile(k, j)

    def turn(k):
        img_t[:, k * R2 : (k + 1) * R2] = img_all[k * R2 : (k + 1) * R2, :].T

    def finish_rows(k):
        for r in range(2):
            rows = slice(k * R2 + r * B, k * R2 + r * B + B)
            m = [rm_ref[j, rows, :] for j in range(4)]
            top = jnp.maximum(jnp.maximum(m[0], m[1]), jnp.maximum(m[2], m[3]))
            e = [rl_ref[j, rows, :] * jnp.exp2(m[j] - top) for j in range(4)]
            v = (top + jnp.log((e[0] + e[1]) + (e[2] + e[3])) * LOG2E).T
            top = jnp.max(v, 0, keepdims=True)
            q = r * NZ + k
            msg_r[q : q + 1, :] = top + jnp.log(jnp.sum(jnp.exp2(v - top), 0, keepdims=True)) * LOG2E

    for i in (1, 3, 2):
        txt_first(i).wait_recv()
        for j in (1, 3, 2):
            txt_second(i, j).start()
    sib_copy(0).wait_recv()
    img_copy(2).wait_recv()
    img_forward(3).start()
    img_forward(4, 0).start()
    img_copy(6).wait_recv()
    img_forward(5).start()
    img_forward(4, 1).start()
    sib_copy(2).start()
    sib_copy(6).start()
    for k in (1, 7):
        img_copy(k).wait_recv()
        sib_copy(k).start()
    tiles((0,), (0,))
    turn(0)
    for k in (2, 6, 1, 7):
        sib_copy(k).wait_recv()
    tiles((2, 6, 1, 7), (0,))
    for k in (2, 6, 1, 7):
        turn(k)
    txt_quarter(1)
    tiles((0, 2, 6, 1, 7), (1,))
    img_forward(3).wait_recv()
    sib_copy(3).start()
    img_forward(5).wait_recv()
    sib_copy(5).start()
    txt_quarter(3)
    tiles((0, 2, 6, 1, 7), (3,))
    img_forward(4, 0).wait_recv()
    img_forward(4, 1).wait_recv()
    sib_copy(4).start()
    sib_copy(3).wait_recv()
    sib_copy(5).wait_recv()
    tiles((3, 5), (0, 1, 3))
    turn(3)
    turn(5)
    txt_quarter(2)
    tiles((0, 2, 6, 1, 7, 3, 5), (2,))
    sib_copy(4).wait_recv()
    tiles((4,), (0, 1, 3, 2))
    turn(4)
    for k in range(NZ):
        finish_rows(k)

    for cc in range(COLS // 128):
        lanes = slice(cc * 128, (cc + 1) * 128)
        mt = cm_ref[:, :, lanes].reshape(NZ * 8, 128)
        lt = cl_ref[:, :, lanes].reshape(NZ * 8, 128)
        top = jnp.max(mt, 0, keepdims=True)
        total = jnp.sum(lt * jnp.exp2(mt - top), 0, keepdims=True)
        msg_c[cc : cc + 1, :] = top + jnp.log(total) * LOG2E

    def row_msg(d, r):
        q = d * 2 + r
        return rcopy(msg_r, got_r.at[q], mr_s, mr_r, dev(0, 0, d, r))

    def col_msg(i, j):
        q = j * 4 + i
        return rcopy(msg_c, got_c.at[q], mc_s, mc_r, dev_ab(i, j))

    for d, r in row_peers:
        row_msg(d, r).start()
    for i, j in col_peers:
        col_msg(i, j).start()

    def combine(parts):
        top = parts[0]
        for p in parts[1:]:
            top = jnp.maximum(top, p)
        total = jnp.exp2(parts[0] - top)
        for p in parts[1:]:
            total = total + jnp.exp2(p - top)
        return top + jnp.log(total) * LOG2E

    drain(got_r.at[pl.ds(1, 15)], mr_r)
    halves = ([], [])
    diag = msg_r[16:24, :]
    for d in range(NZ):
        for r in range(2):
            ref = msg_r if (d, r) == (0, 0) else got_r.at[d * 2 + r]
            if (d, r) != (0, 0):
                diag = diag + ref[16:24, :]
            for rs in range(2):
                v = ref[rs * 8 : rs * 8 + 8, :]
                halves[rs ^ r].append(pltpu.roll(v, d, 0) if d else v)
    lr = [combine(h) for h in halves]

    drain(got_c.at[pl.ds(1, 15)], mc_r)
    jj = lax.broadcasted_iota(jnp.int32, (NX * NY, 128), 0) % NY
    parts = []
    for a in range(NX):
        for b in range(NY):
            v = msg_c[...] if (a, b) == (0, 0) else got_c[a * NY + b]
            s1, s2 = (4 * a + b) % 16, (4 * a + b + 12) % 16
            if b == 0:
                v = pltpu.roll(v, s1, 0) if s1 else v
            else:
                v = jnp.where(jj >= b, pltpu.roll(v, s1, 0), pltpu.roll(v, s2, 0) if s2 else v)
            parts.append(v)
    lc = combine(parts)
    lc_ref[...] = lc + 1.0

    out_a[...] = (lr[0] + lr[1]) * LN2 - (2.0 * factor) * diag
    out_b[...] = (lc[0:8] + lc[8:16]) * LN2

    def a_msg(i, j):
        q = j * 4 + i
        return rcopy(out_a, got_a.at[q], la_s, la_r, dev_ab(i, j))

    def b_msg(d, r):
        q = d * 2 + r
        return rcopy(out_b, got_b.at[q], lb_s, lb_r, dev(0, 0, d, r))

    for i, j in col_peers:
        a_msg(i, j).start()
    for d, r in row_peers:
        b_msg(d, r).start()

    for k in range(NZ):
        for r in range(2):
            lrb_ref[k * R2 + r * B : k * R2 + (r + 1) * B, :] = (
                jnp.broadcast_to(lr[r][k : k + 1, :], (B, 128)) + 1.0
            ).T

    def sib_part(k):
        return rcopy(sib_out.at[k], sib_in.at[k], sb_s, sb_r.at[k], dev(0, 0, 0, 1))

    def far_part(k):
        if k == 3:
            return rcopy(far_out.at[3], mid_in.at[0], fo_s, fo_r.at[3], dev(0, 0, -1, 0))
        if k == 5:
            return rcopy(far_out.at[5], mid_in.at[1], fo_s, fo_r.at[5], dev(0, 0, 1, 0))
        if k == 4:
            rows = pl.ds(0, 64)
            return rcopy(far_out.at[4, rows], mid_in.at[2, rows], fo_s, fo_r.at[4], dev(0, 0, -2, 0))
        if k == 8:
            rows = pl.ds(64, 64)
            return rcopy(far_out.at[4, rows], mid_in.at[2, rows], fo_s, fo_r.at[8], dev(0, 0, 2, 0))
        return rcopy(far_out.at[k], far_in.at[k], fo_s, fo_r.at[k], dev(0, 0, -k, 0))

    def pass_on(k):
        sib_part(k).wait_recv()
        total = keep_i[k] + sib_in[k]
        if k in (2, 6):
            half = 0 if k == 2 else 1
            far_part(3 if k == 2 else 5).wait_recv()
            far_part(4 if k == 2 else 8).wait_recv()
            total = total + mid_in[half].astype(F32)
            h = slice(half * 64, half * 64 + 64)
            far_out[k] = total.astype(BF16)
            far_out[k, h, :] = (total[h] + mid_in[2, h, :].astype(F32)).astype(BF16)
        else:
            far_out[k] = total.astype(BF16)
        far_part(k).start()
        if k == 4:
            far_part(8).start()

    def weigh(k, js):
        rows = slice(k * R2, (k + 1) * R2)
        for j in js:
            for cc in range(j * 4, j * 4 + 4):
                lanes = slice(cc * 128, (cc + 1) * 128)
                s = s_ref[rows, lanes]
                w = jnp.exp2(s - lrb_ref[rows, :]) + jnp.exp2(s - lc_ref[cc : cc + 1, :])
                w_ref[rows, lanes] = w.astype(BF16)

    def txt_part(j):
        return rcopy(t_out.at[j], t_in.at[j], to_s, to_r.at[j], dev_ab(0, -j))

    def txt_part2(i):
        return rcopy(u_out.at[i], u_in.at[i], uo_s, to_r.at[4 + i], dev_ab(-i, 0))

    def third(j):
        return jnp.dot(img_t[...], w_ref[:, j * QC : (j + 1) * QC], preferred_element_type=F32)

    def send_quarter(j):
        t_out[j] = third(j).astype(BF16)
        txt_part(j).start()

    for j in (2, 1):
        for k in range(NZ):
            weigh(k, (j,))
        send_quarter(j)

    ks = (4, 3, 5, 1, 7, 2, 6, 0)
    weigh(ks[0], (0, 3))
    for n, k in enumerate(ks):
        if n < 7:
            weigh(ks[n + 1], (0, 3))
        part = jnp.dot(w_ref[k * R2 : (k + 1) * R2, :], txt_all[...], preferred_element_type=F32)
        keep_i[k] = part[0:B]
        sib_out[k] = part[B:R2]
        sib_part(k).start()
        if 1 <= n <= 5:
            pass_on(ks[n - 1])
    send_quarter(3)
    pass_on(2)
    pass_on(6)
    keep_t[...] = third(0)

    drain(got_a.at[pl.ds(1, 15)], la_r)
    drain(got_b.at[pl.ds(1, 15)], lb_r)
    share = out_a[...] + out_b[...]
    for q in range(1, 16):
        share = share + got_a[q] + got_b[q]
    loss_ref[0] = jnp.sum(share) / (2.0 * 256 * B)

    for j in (2, 1, 3):
        txt_part(j).wait_recv()
    for i in (2, 1, 3, 0):
        h = slice(i * B, (i + 1) * B)
        total = keep_t[:, h] + t_in[1, :, h].astype(F32) + t_in[2, :, h].astype(F32) + t_in[3, :, h].astype(F32)
        if i:
            u_out[i] = total.astype(BF16)
            txt_part2(i).start()
        else:
            own_t = total

    sib_part(0).wait_recv()
    total = keep_i[0] + sib_in[0]
    for k in (1, 7, 2, 6):
        far_part(k).wait_recv()
        total = total + far_in[k].astype(F32)
    gi_ref[...] = factor * (total - txt_ref[...].astype(F32))

    for i in (1, 3, 2):
        txt_part2(i).wait_recv()
        own_t = own_t + u_in[i].astype(F32)
    gt_ref[...] = factor * (own_t.T - img_ref[...].astype(F32))

    drain(txt_all.at[pl.ds(0, 15 * B)], ts_s)
    drain(img_all.at[pl.ds(0, 7 * B)], is_s)
    drain(img_all.at[pl.ds(0, 8 * B)], fs_s)
    drain(got_r.at[pl.ds(1, 15)], mr_s)
    drain(got_c.at[pl.ds(1, 15)], mc_s)
    drain(got_a.at[pl.ds(1, 15)], la_s)
    drain(got_b.at[pl.ds(1, 15)], lb_s)
    drain(sib_in, sb_s)
    drain(far_in.at[pl.ds(1, 7)], fo_s)
    drain(t_in.at[pl.ds(1, 3)], to_s)
    drain(u_in.at[pl.ds(1, 3)], uo_s)


def local(images, texts, logit_scale):
    dma = pltpu.SemaphoreType.DMA
    vm = pltpu.VMEM
    return pl.pallas_call(
        kernel,
        out_shape=(
            jax.ShapeDtypeStruct((1,), F32),
            jax.ShapeDtypeStruct((B, E), F32),
            jax.ShapeDtypeStruct((B, E), F32),
        ),
        in_specs=[
            pl.BlockSpec(memory_space=pltpu.SMEM),
            pl.BlockSpec(memory_space=vm),
            pl.BlockSpec(memory_space=vm),
        ],
        out_specs=(
            pl.BlockSpec(memory_space=pltpu.SMEM),
            pl.BlockSpec(memory_space=vm),
            pl.BlockSpec(memory_space=vm),
        ),
        scratch_shapes=[
            vm((ROWS, E), BF16), vm((COLS, E), BF16), vm((E, ROWS), BF16),
            vm((ROWS, COLS), F32), vm((ROWS, COLS), BF16),
            vm((4, ROWS, 128), F32), vm((4, ROWS, 128), F32), vm((NZ, 8, COLS), F32), vm((NZ, 8, COLS), F32),
            vm((ROWS, 128), F32), vm((16, 128), F32),
            vm((24, 128), F32), vm((16, 128), F32), vm((16, 24, 128), F32), vm((16, 16, 128), F32),
            vm((8, 128), F32), vm((8, 128), F32), vm((16, 8, 128), F32), vm((16, 8, 128), F32),
            vm((NZ, B, E), F32), vm((NZ, B, E), F32), vm((NZ, B, E), F32),
            vm((NZ, B, E), BF16), vm((NZ, B, E), BF16), vm((3, B, E), BF16),
            vm((E, QC), F32), vm((4, E, QC), BF16), vm((4, E, QC), BF16), vm((4, E, B), BF16), vm((4, E, B), BF16),
            dma, dma((9,)), dma, dma((NZ,)), dma, dma((7,)),
            dma, dma, dma, dma, dma, dma, dma, dma,
            dma, dma((NZ,)), dma, dma((9,)), dma, dma, dma((8,)),
        ],
        compiler_params=pltpu.CompilerParams(
            collective_id=0, has_side_effects=True, vmem_limit_bytes=56 * 1024 * 1024
        ),
        cost_estimate=pl.CostEstimate(
            flops=6 * ROWS * COLS * E, bytes_accessed=8 * B * E, transcendentals=4 * ROWS * COLS
        ),
    )(logit_scale, images, texts)


def solution(mesh):
    spec = P(("outer", "inner"), None)
    return jax.shard_map(
        local, mesh=mesh, in_specs=(spec, spec, P()), out_specs=(P(), spec, spec), check_vma=False
    )
```

```python
import math

import jax
import jax.numpy as jnp
from jax import lax
from jax.experimental import pallas as pl
from jax.experimental.pallas import tpu as pltpu
from jax.sharding import PartitionSpec as P

MESH = pl.DeviceIdType.MESH
F32 = jnp.float32
BF16 = jnp.bfloat16
B = 128
E = 384
NX, NY, NZ = 4, 4, 8
ROWS = NZ * 2 * B
COLS = NX * NY * B
R2 = 2 * B
QC = 4 * B
LOG2E = math.log2(math.e)
LN2 = math.log(2.0)


def nt(a, b):
    return lax.dot_general(a, b, (((1,), (1,)), ((), ())), preferred_element_type=F32)


def kernel(
    scale_ref, img_ref, txt_ref, loss_ref, gi_ref, gt_ref,
    img_all, txt_all, img_t, s_ref, w_ref,
    rm_ref, rl_ref, cm_ref, cl_ref, lrb_ref, lc_ref,
    msg_r, msg_c, got_r, got_c, out_a, out_b, got_a, got_b,
    keep_i, sib_out, sib_in, far_out, far_in, mid_in, keep_t, t_out, t_in, u_out, u_in,
    is_s, is_r, fs_s, fs_r, ts_s, ts_r, mr_s, mr_r, mc_s, mc_r,
    la_s, la_r, lb_s, lb_r, sb_s, sb_r, fo_s, fo_r, to_s, uo_s, to_r,
):
    outer, inner = lax.axis_index("outer"), lax.axis_index("inner")
    c = outer % 2
    x = (outer // 2) % NX
    y = (outer // (2 * NX)) * 2 + inner // NZ
    z = inner % NZ
    factor = scale_ref[0]
    f2 = factor * LOG2E

    def dev(dx, dy, dz, dc):
        xx, yy, zz = (x + dx + NX) % NX, (y + dy + NY) % NY, (z + dz + NZ) % NZ
        cc = (c + dc) % 2
        return ((yy // 2) * (2 * NX) + xx * 2 + cc, (yy % 2) * NZ + zz)

    def dev_ab(da, db):
        return dev(jnp.where(c == 0, da, db), jnp.where(c == 0, db, da), 0, 0)

    def rcopy(src, dst, ss, rs, to):
        return pltpu.make_async_remote_copy(
            src_ref=src, dst_ref=dst, send_sem=ss, recv_sem=rs, device_id=to, device_id_type=MESH
        )

    def drain(ref, sem):
        pltpu.make_async_copy(ref, ref, sem).wait()

    barrier = pltpu.get_barrier_semaphore()
    row_peers = [(d, r) for d in range(NZ) for r in range(2) if (d, r) != (0, 0)]
    col_peers = [(i, j) for i in range(NX) for j in range(NY) if (i, j) != (0, 0)]
    for d, r in row_peers:
        pl.semaphore_signal(barrier, inc=1, device_id=dev(0, 0, d, r), device_id_type=MESH)
    for i, j in col_peers:
        pl.semaphore_signal(barrier, inc=1, device_id=dev_ab(i, j), device_id_type=MESH)
    pl.semaphore_wait(barrier, len(row_peers) + len(col_peers))

    def img_rows(k, h=None):
        return img_all.at[pl.ds(k * R2, B)] if h is None else img_all.at[pl.ds(k * R2 + h * 64, 64)]

    def img_copy(k):
        return rcopy(img_ref, img_rows(k), is_s, is_r.at[k], dev(0, 0, k, 0))

    def img_forward(k, h=None):
        if k == 3:
            return rcopy(img_rows(2), img_rows(3), is_s, is_r.at[3], dev(0, 0, 1, 0))
        if k == 5:
            return rcopy(img_rows(6), img_rows(5), is_s, is_r.at[5], dev(0, 0, -1, 0))
        if h == 0:
            return rcopy(img_rows(2, 0), img_rows(4, 0), is_s, is_r.at[4], dev(0, 0, 2, 0))
        return rcopy(img_rows(6, 1), img_rows(4, 1), is_s, is_r.at[8], dev(0, 0, -2, 0))

    def sib_copy(k):
        return rcopy(img_rows(k), img_all.at[pl.ds(k * R2 + B, B)], fs_s, fs_r.at[k], dev(0, 0, 0, 1))

    def txt_first(i):
        return rcopy(txt_ref, txt_all.at[pl.ds(i * B, B)], ts_s, ts_r.at[i], dev_ab(i, 0))

    def txt_second(i, j):
        return rcopy(
            txt_all.at[pl.ds(i * B, B)], txt_all.at[pl.ds((j * 4 + i) * B, B)], ts_s, ts_r.at[3 + j], dev_ab(0, j)
        )

    def txt_quarter(j):
        drain(txt_all.at[pl.ds(j * QC, QC)], ts_r.at[3 + j])

    img_all[0:B, :] = img_ref[...]
    txt_all[0:B, :] = txt_ref[...]
    for i in (1, 3, 2):
        txt_first(i).start()
    for k in (2, 6, 1, 7):
        img_copy(k).start()
    for j in (1, 3, 2):
        txt_second(0, j).start()
    sib_copy(0).start()

    prod = img_ref[...].astype(F32) * txt_ref[...].astype(F32)
    prod = prod[:, 0:128] + prod[:, 128:256] + prod[:, 256:384]
    msg_c[16:24, :] = jnp.sum(prod.reshape(B // 8, 8, 128), 0)

    def tile(k, j):
        row0 = k * R2
        block = img_all[row0 : row0 + R2, :]
        for cc in range(j * 2, j * 2 + 2):
            s = nt(block, txt_all[cc * 256 : (cc + 1) * 256, :]) * f2
            s_ref[row0 : row0 + R2, cc * 256 : (cc + 1) * 256] = s
        for cc in range(j * 4, j * 4 + 4):
            lanes = slice(cc * 128, (cc + 1) * 128)
            slab = s_ref[row0 : row0 + R2, lanes].reshape(R2 // 8, 8, 128)
            top = jnp.max(slab, 0)
            cm_ref[k, :, lanes] = top
            cl_ref[k, :, lanes] = jnp.sum(jnp.exp2(slab - top[None]), 0)
        for rr in range(R2 // 32):
            rows = slice(row0 + rr * 32, row0 + rr * 32 + 32)
            parts = [s_ref[rows, cc * 128 : (cc + 1) * 128] for cc in range(j * 4, j * 4 + 4)]
            top = jnp.maximum(jnp.maximum(parts[0], parts[1]), jnp.maximum(parts[2], parts[3]))
            e = [jnp.exp2(p - top) for p in parts]
            rm_ref[j, rows, :] = top
            rl_ref[j, rows, :] = (e[0] + e[1]) + (e[2] + e[3])

    def tiles(ks, js):
        for j in js:
            for k in ks:
                tile(k, j)

    def turn(k):
        img_t[:, k * R2 : (k + 1) * R2] = img_all[k * R2 : (k + 1) * R2, :].T

    def finish_rows(k):
        for r in range(2):
            rows = slice(k * R2 + r * B, k * R2 + r * B + B)
            m = [rm_ref[j, rows, :] for j in range(4)]
            top = jnp.maximum(jnp.maximum(m[0], m[1]), jnp.maximum(m[2], m[3]))
            e = [rl_ref[j, rows, :] * jnp.exp2(m[j] - top) for j in range(4)]
            v = (top + jnp.log((e[0] + e[1]) + (e[2] + e[3])) * LOG2E).T
            top = jnp.max(v, 0, keepdims=True)
            q = r * NZ + k
            msg_r[q : q + 1, :] = top + jnp.log(jnp.sum(jnp.exp2(v - top), 0, keepdims=True)) * LOG2E

    for i in (1, 3, 2):
        txt_first(i).wait_recv()
        for j in (1, 3, 2):
            txt_second(i, j).start()
    sib_copy(0).wait_recv()
    img_copy(2).wait_recv()
    img_forward(3).start()
    img_forward(4, 0).start()
    img_copy(6).wait_recv()
    img_forward(5).start()
    img_forward(4, 1).start()
    sib_copy(2).start()
    sib_copy(6).start()
    for k in (1, 7):
        img_copy(k).wait_recv()
        sib_copy(k).start()
    tiles((0,), (0,))
    turn(0)
    for k in (2, 6, 1, 7):
        sib_copy(k).wait_recv()
    tiles((2, 6, 1, 7), (0,))
    for k in (2, 6, 1, 7):
        turn(k)
    txt_quarter(1)
    tiles((0, 2, 6, 1, 7), (1,))
    img_forward(3).wait_recv()
    sib_copy(3).start()
    img_forward(5).wait_recv()
    sib_copy(5).start()
    txt_quarter(3)
    tiles((0, 2, 6, 1, 7), (3,))
    img_forward(4, 0).wait_recv()
    img_forward(4, 1).wait_recv()
    sib_copy(4).start()
    sib_copy(3).wait_recv()
    sib_copy(5).wait_recv()
    tiles((3, 5), (0, 1, 3))
    turn(3)
    turn(5)
    txt_quarter(2)
    tiles((0, 2, 6, 1, 7, 3, 5), (2,))
    sib_copy(4).wait_recv()
    tiles((4,), (0, 1, 3, 2))
    turn(4)
    for k in range(NZ):
        finish_rows(k)

    def row_msg(d, r):
        return rcopy(msg_r, got_r.at[d * 2 + r], mr_s, mr_r, dev(0, 0, d, r))

    def col_msg(i, j):
        return rcopy(msg_c, got_c.at[j * 4 + i], mc_s, mc_r, dev_ab(i, j))

    def a_msg(i, j):
        return rcopy(out_a, got_a.at[j * 4 + i], la_s, la_r, dev_ab(i, j))

    def b_msg(d, r):
        return rcopy(out_b, got_b.at[d * 2 + r], lb_s, lb_r, dev(0, 0, d, r))

    def combine(parts):
        top = parts[0]
        for p in parts[1:]:
            top = jnp.maximum(top, p)
        total = jnp.exp2(parts[0] - top)
        for p in parts[1:]:
            total = total + jnp.exp2(p - top)
        return top + jnp.log(total) * LOG2E

    for d in (4, 3, 5, 2, 6, 1, 7, 0):
        for r in range(2):
            if (d, r) != (0, 0):
                row_msg(d, r).start()

    for cc in range(COLS // 128):
        lanes = slice(cc * 128, (cc + 1) * 128)
        mt = cm_ref[:, :, lanes].reshape(NZ * 8, 128)
        lt = cl_ref[:, :, lanes].reshape(NZ * 8, 128)
        top = jnp.max(mt, 0, keepdims=True)
        total = jnp.sum(lt * jnp.exp2(mt - top), 0, keepdims=True)
        msg_c[cc : cc + 1, :] = top + jnp.log(total) * LOG2E

    for i, j in reversed(col_peers):
        col_msg(i, j).start()

    drain(got_r.at[pl.ds(1, 15)], mr_r)
    halves = ([], [])
    for d in range(NZ):
        for r in range(2):
            ref = msg_r if (d, r) == (0, 0) else got_r.at[d * 2 + r]
            for rs in range(2):
                v = ref[rs * 8 : rs * 8 + 8, :]
                halves[rs ^ r].append(pltpu.roll(v, d, 0) if d else v)
    lr = [combine(h) for h in halves]
    for k in range(NZ):
        for r in range(2):
            lrb_ref[k * R2 + r * B : k * R2 + (r + 1) * B, :] = (
                jnp.broadcast_to(lr[r][k : k + 1, :], (B, 128)) + 1.0
            ).T

    drain(got_c.at[pl.ds(1, 15)], mc_r)
    jj = lax.broadcasted_iota(jnp.int32, (NX * NY, 128), 0) % NY
    parts = []
    diag = msg_c[16:24, :]
    for a in range(NX):
        for b in range(NY):
            ref = msg_c if (a, b) == (0, 0) else got_c.at[a * NY + b]
            v = ref[0:16, :]
            if (a, b) != (0, 0):
                diag = diag + ref[16:24, :]
            s1, s2 = (4 * a + b) % 16, (4 * a + b + 12) % 16
            if b == 0:
                v = pltpu.roll(v, s1, 0) if s1 else v
            else:
                v = jnp.where(jj >= b, pltpu.roll(v, s1, 0), pltpu.roll(v, s2, 0) if s2 else v)
            parts.append(v)
    lc = combine(parts)
    lc_ref[...] = lc + 1.0

    out_a[...] = (lr[0] + lr[1]) * LN2
    out_b[...] = (lc[0:8] + lc[8:16]) * LN2 - (2.0 * factor) * diag

    def send_shares():
        for i, j in col_peers:
            a_msg(i, j).start()
        for d, r in row_peers:
            b_msg(d, r).start()

    def sib_part(k):
        return rcopy(sib_out.at[k], sib_in.at[k], sb_s, sb_r.at[k], dev(0, 0, 0, 1))

    def far_part(k):
        if k == 3:
            return rcopy(far_out.at[3], mid_in.at[0], fo_s, fo_r.at[3], dev(0, 0, -1, 0))
        if k == 5:
            return rcopy(far_out.at[5], mid_in.at[1], fo_s, fo_r.at[5], dev(0, 0, 1, 0))
        if k == 4:
            rows = pl.ds(0, 64)
            return rcopy(far_out.at[4, rows], mid_in.at[2, rows], fo_s, fo_r.at[4], dev(0, 0, -2, 0))
        if k == 8:
            rows = pl.ds(64, 64)
            return rcopy(far_out.at[4, rows], mid_in.at[2, rows], fo_s, fo_r.at[8], dev(0, 0, 2, 0))
        return rcopy(far_out.at[k], far_in.at[k], fo_s, fo_r.at[k], dev(0, 0, -k, 0))

    def pass_on(k):
        sib_part(k).wait_recv()
        total = keep_i[k] + sib_in[k]
        if k in (2, 6):
            half = 0 if k == 2 else 1
            far_part(3 if k == 2 else 5).wait_recv()
            far_part(4 if k == 2 else 8).wait_recv()
            total = total + mid_in[half].astype(F32)
            h = slice(half * 64, half * 64 + 64)
            far_out[k] = total.astype(BF16)
            far_out[k, h, :] = (total[h] + mid_in[2, h, :].astype(F32)).astype(BF16)
        else:
            far_out[k] = total.astype(BF16)
        far_part(k).start()
        if k == 4:
            far_part(8).start()

    def weigh(k, js):
        rows = slice(k * R2, (k + 1) * R2)
        for j in js:
            for cc in range(j * 4, j * 4 + 4):
                lanes = slice(cc * 128, (cc + 1) * 128)
                s = s_ref[rows, lanes]
                w = jnp.exp2(s - lrb_ref[rows, :]) + jnp.exp2(s - lc_ref[cc : cc + 1, :])
                w_ref[rows, lanes] = w.astype(BF16)

    def txt_part(j):
        return rcopy(t_out.at[j], t_in.at[j], to_s, to_r.at[j], dev_ab(0, -j))

    def txt_part2(i):
        return rcopy(u_out.at[i], u_in.at[i], uo_s, to_r.at[4 + i], dev_ab(-i, 0))

    def third(j):
        return jnp.dot(img_t[...], w_ref[:, j * QC : (j + 1) * QC], preferred_element_type=F32)

    def send_quarter(j):
        t_out[j] = third(j).astype(BF16)
        txt_part(j).start()

    for k in range(NZ):
        weigh(k, (2,))
    send_quarter(2)
    send_shares()
    for k in range(NZ):
        weigh(k, (1,))
    send_quarter(1)
    for k in range(NZ):
        weigh(k, (3,))
    send_quarter(3)

    ks = (4, 3, 5, 1, 7, 2, 6, 0)
    weigh(ks[0], (0,))
    for n, k in enumerate(ks):
        if n < 7:
            weigh(ks[n + 1], (0,))
        part = jnp.dot(w_ref[k * R2 : (k + 1) * R2, :], txt_all[...], preferred_element_type=F32)
        keep_i[k] = part[0:B]
        sib_out[k] = part[B:R2]
        sib_part(k).start()
        if 1 <= n <= 5:
            pass_on(ks[n - 1])
    pass_on(2)
    pass_on(6)
    keep_t[...] = third(0)

    drain(got_a.at[pl.ds(1, 15)], la_r)
    drain(got_b.at[pl.ds(1, 15)], lb_r)
    share = out_a[...] + out_b[...]
    for q in range(1, 16):
        share = share + got_a[q] + got_b[q]
    loss_ref[0] = jnp.sum(share) / (2.0 * 256 * B)

    for j in (2, 1, 3):
        txt_part(j).wait_recv()
    for i in (2, 1, 3, 0):
        h = slice(i * B, (i + 1) * B)
        total = keep_t[:, h] + t_in[1, :, h].astype(F32) + t_in[2, :, h].astype(F32) + t_in[3, :, h].astype(F32)
        if i:
            u_out[i] = total.astype(BF16)
            txt_part2(i).start()
        else:
            own_t = total

    sib_part(0).wait_recv()
    total = keep_i[0] + sib_in[0]
    for k in (1, 7, 2, 6):
        far_part(k).wait_recv()
        total = total + far_in[k].astype(F32)
    gi_ref[...] = factor * (total - txt_ref[...].astype(F32))

    for i in (1, 3, 2):
        txt_part2(i).wait_recv()
        own_t = own_t + u_in[i].astype(F32)
    gt_ref[...] = factor * (own_t.T - img_ref[...].astype(F32))

    drain(txt_all.at[pl.ds(0, 15 * B)], ts_s)
    drain(img_all.at[pl.ds(0, 7 * B)], is_s)
    drain(img_all.at[pl.ds(0, 8 * B)], fs_s)
    drain(got_r.at[pl.ds(1, 15)], mr_s)
    drain(got_c.at[pl.ds(1, 15)], mc_s)
    drain(got_a.at[pl.ds(1, 15)], la_s)
    drain(got_b.at[pl.ds(1, 15)], lb_s)
    drain(sib_in, sb_s)
    drain(far_in.at[pl.ds(1, 7)], fo_s)
    drain(t_in.at[pl.ds(1, 3)], to_s)
    drain(u_in.at[pl.ds(1, 3)], uo_s)


def hand_over(loss_in, gi_in, gt_in, loss_ref, gi_ref, gt_ref):
    loss_ref[0] = loss_in[0]
    gi_ref[...] = gi_in[...]
    gt_ref[...] = gt_in[...]


def local(images, texts, logit_scale):
    dma = pltpu.SemaphoreType.DMA
    vm = pltpu.VMEM
    parts = pl.pallas_call(
        kernel,
        out_shape=(
            jax.ShapeDtypeStruct((1,), F32),
            jax.ShapeDtypeStruct((B, E), F32),
            jax.ShapeDtypeStruct((B, E), F32),
        ),
        in_specs=[
            pl.BlockSpec(memory_space=pltpu.SMEM),
            pl.BlockSpec(memory_space=vm),
            pl.BlockSpec(memory_space=vm),
        ],
        out_specs=(
            pl.BlockSpec(memory_space=pltpu.SMEM),
            pl.BlockSpec(memory_space=vm),
            pl.BlockSpec(memory_space=vm),
        ),
        scratch_shapes=[
            vm((ROWS, E), BF16), vm((COLS, E), BF16), vm((E, ROWS), BF16),
            vm((ROWS, COLS), F32), vm((ROWS, COLS), BF16),
            vm((4, ROWS, 128), F32), vm((4, ROWS, 128), F32), vm((NZ, 8, COLS), F32), vm((NZ, 8, COLS), F32),
            vm((ROWS, 128), F32), vm((16, 128), F32),
            vm((16, 128), F32), vm((24, 128), F32), vm((16, 16, 128), F32), vm((16, 24, 128), F32),
            vm((8, 128), F32), vm((8, 128), F32), vm((16, 8, 128), F32), vm((16, 8, 128), F32),
            vm((NZ, B, E), F32), vm((NZ, B, E), F32), vm((NZ, B, E), F32),
            vm((NZ, B, E), BF16), vm((NZ, B, E), BF16), vm((3, B, E), BF16),
            vm((E, QC), F32), vm((4, E, QC), BF16), vm((4, E, QC), BF16), vm((4, E, B), BF16), vm((4, E, B), BF16),
            dma, dma((9,)), dma, dma((NZ,)), dma, dma((7,)),
            dma, dma, dma, dma, dma, dma, dma, dma,
            dma, dma((NZ,)), dma, dma((9,)), dma, dma, dma((8,)),
        ],
        compiler_params=pltpu.CompilerParams(
            collective_id=0, has_side_effects=True, vmem_limit_bytes=56 * 1024 * 1024
        ),
        cost_estimate=pl.CostEstimate(
            flops=6 * ROWS * COLS * E, bytes_accessed=8 * B * E, transcendentals=4 * ROWS * COLS
        ),
    )(logit_scale, images, texts)
    return pl.pallas_call(
        hand_over,
        out_shape=(
            jax.ShapeDtypeStruct((1,), F32),
            jax.ShapeDtypeStruct((B, E), F32),
            jax.ShapeDtypeStruct((B, E), F32),
        ),
        in_specs=[pl.BlockSpec(memory_space=pltpu.SMEM), pl.BlockSpec(memory_space=vm), pl.BlockSpec(memory_space=vm)],
        out_specs=(
            pl.BlockSpec(memory_space=pltpu.SMEM), pl.BlockSpec(memory_space=vm), pl.BlockSpec(memory_space=vm)
        ),
    )(*parts)


def solution(mesh):
    spec = P(("outer", "inner"), None)
    return jax.shard_map(
        local, mesh=mesh, in_specs=(spec, spec, P()), out_specs=(P(), spec, spec), check_vma=False
    )
```

```python
import math

import jax
import jax.numpy as jnp
from jax import lax
from jax.experimental import pallas as pl
from jax.experimental.pallas import tpu as pltpu
from jax.sharding import PartitionSpec as P

MESH = pl.DeviceIdType.MESH
F32 = jnp.float32
BF16 = jnp.bfloat16
B = 128
E = 384
NX, NY, NZ = 4, 4, 8
ROWS = NZ * 2 * B
COLS = NX * NY * B
R2 = 2 * B
QC = 4 * B
LOG2E = math.log2(math.e)
LN2 = math.log(2.0)


def nt(a, b):
    return lax.dot_general(a, b, (((1,), (1,)), ((), ())), preferred_element_type=F32)


def kernel(
    scale_ref, img_ref, txt_ref, loss_ref, gi_ref, gt_ref,
    img_all, txt_all, img_t, s_ref, w_ref,
    rm_ref, rl_ref, cm_ref, cl_ref, lrb_ref, lc_ref,
    msg_r, msg_c, got_r, got_c, out_a, out_b, got_a, got_b,
    keep_i, sib_out, sib_in, far_out, far_in, mid_in, keep_t, t_out, t_in, u_out, u_in,
    is_s, is_r, fs_s, fs_r, ts_s, ts_r, mr_s, mr_r, mc_s, mc_r,
    la_s, la_r, lb_s, lb_r, sb_s, sb_r, fo_s, fo_r, to_s, uo_s, to_r,
):
    outer, inner = lax.axis_index("outer"), lax.axis_index("inner")
    c = outer % 2
    x = (outer // 2) % NX
    y = (outer // (2 * NX)) * 2 + inner // NZ
    z = inner % NZ
    factor = scale_ref[0]
    f2 = factor * LOG2E

    def dev(dx, dy, dz, dc):
        xx, yy, zz = (x + dx + NX) % NX, (y + dy + NY) % NY, (z + dz + NZ) % NZ
        cc = (c + dc) % 2
        return ((yy // 2) * (2 * NX) + xx * 2 + cc, (yy % 2) * NZ + zz)

    def dev_ab(da, db):
        return dev(jnp.where(c == 0, da, db), jnp.where(c == 0, db, da), 0, 0)

    def rcopy(src, dst, ss, rs, to):
        return pltpu.make_async_remote_copy(
            src_ref=src, dst_ref=dst, send_sem=ss, recv_sem=rs, device_id=to, device_id_type=MESH
        )

    def drain(ref, sem):
        pltpu.make_async_copy(ref, ref, sem).wait()

    barrier = pltpu.get_barrier_semaphore()
    row_peers = [(d, r) for d in range(NZ) for r in range(2) if (d, r) != (0, 0)]
    col_peers = [(i, j) for i in range(NX) for j in range(NY) if (i, j) != (0, 0)]
    for d, r in row_peers:
        pl.semaphore_signal(barrier, inc=1, device_id=dev(0, 0, d, r), device_id_type=MESH)
    for i, j in col_peers:
        pl.semaphore_signal(barrier, inc=1, device_id=dev_ab(i, j), device_id_type=MESH)
    pl.semaphore_wait(barrier, len(row_peers) + len(col_peers))

    def img_rows(k, h=None):
        return img_all.at[pl.ds(k * R2, B)] if h is None else img_all.at[pl.ds(k * R2 + h * 64, 64)]

    def img_copy(k):
        return rcopy(img_ref, img_rows(k), is_s, is_r.at[k], dev(0, 0, k, 0))

    def img_forward(k, h=None):
        if k == 3:
            return rcopy(img_rows(2), img_rows(3), is_s, is_r.at[3], dev(0, 0, 1, 0))
        if k == 5:
            return rcopy(img_rows(6), img_rows(5), is_s, is_r.at[5], dev(0, 0, -1, 0))
        if h == 0:
            return rcopy(img_rows(2, 0), img_rows(4, 0), is_s, is_r.at[4], dev(0, 0, 2, 0))
        return rcopy(img_rows(6, 1), img_rows(4, 1), is_s, is_r.at[8], dev(0, 0, -2, 0))

    def sib_copy(k):
        return rcopy(img_rows(k), img_all.at[pl.ds(k * R2 + B, B)], fs_s, fs_r.at[k], dev(0, 0, 0, 1))

    def txt_first(i):
        return rcopy(txt_ref, txt_all.at[pl.ds(i * B, B)], ts_s, ts_r.at[i], dev_ab(i, 0))

    def txt_second(i, j):
        return rcopy(
            txt_all.at[pl.ds(i * B, B)], txt_all.at[pl.ds((j * 4 + i) * B, B)], ts_s, ts_r.at[3 + j], dev_ab(0, j)
        )

    def txt_quarter(j):
        drain(txt_all.at[pl.ds(j * QC, QC)], ts_r.at[3 + j])

    img_all[0:B, :] = img_ref[...]
    txt_all[0:B, :] = txt_ref[...]
    for i in (1, 3, 2):
        txt_first(i).start()
    for k in (2, 6, 1, 7):
        img_copy(k).start()
    for j in (1, 3):
        txt_second(0, j).start()
    sib_copy(0).start()

    prod = img_ref[...].astype(F32) * txt_ref[...].astype(F32)
    prod = prod[:, 0:128] + prod[:, 128:256] + prod[:, 256:384]
    msg_c[16:24, :] = jnp.sum(prod.reshape(B // 8, 8, 128), 0)

    def tile(k, j):
        row0 = k * R2
        block = img_all[row0 : row0 + R2, :]
        for cc in range(j * 2, j * 2 + 2):
            s = nt(block, txt_all[cc * 256 : (cc + 1) * 256, :]) * f2
            s_ref[row0 : row0 + R2, cc * 256 : (cc + 1) * 256] = s
        for cc in range(j * 4, j * 4 + 4):
            lanes = slice(cc * 128, (cc + 1) * 128)
            slab = s_ref[row0 : row0 + R2, lanes].reshape(R2 // 8, 8, 128)
            top = jnp.max(slab, 0)
            cm_ref[k, :, lanes] = top
            cl_ref[k, :, lanes] = jnp.sum(jnp.exp2(slab - top[None]), 0)
        for rr in range(R2 // 32):
            rows = slice(row0 + rr * 32, row0 + rr * 32 + 32)
            parts = [s_ref[rows, cc * 128 : (cc + 1) * 128] for cc in range(j * 4, j * 4 + 4)]
            top = jnp.maximum(jnp.maximum(parts[0], parts[1]), jnp.maximum(parts[2], parts[3]))
            e = [jnp.exp2(p - top) for p in parts]
            rm_ref[j, rows, :] = top
            rl_ref[j, rows, :] = (e[0] + e[1]) + (e[2] + e[3])

    def tiles(ks, js):
        for j in js:
            for k in ks:
                tile(k, j)

    def turn(k):
        img_t[:, k * R2 : (k + 1) * R2] = img_all[k * R2 : (k + 1) * R2, :].T

    def finish_rows(k):
        for r in range(2):
            rows = slice(k * R2 + r * B, k * R2 + r * B + B)
            m = [rm_ref[j, rows, :] for j in range(4)]
            top = jnp.maximum(jnp.maximum(m[0], m[1]), jnp.maximum(m[2], m[3]))
            e = [rl_ref[j, rows, :] * jnp.exp2(m[j] - top) for j in range(4)]
            v = (top + jnp.log((e[0] + e[1]) + (e[2] + e[3])) * LOG2E).T
            top = jnp.max(v, 0, keepdims=True)
            q = r * NZ + k
            msg_r[q : q + 1, :] = top + jnp.log(jnp.sum(jnp.exp2(v - top), 0, keepdims=True)) * LOG2E

    for i in (1, 3, 2):
        txt_first(i).wait_recv()
        for j in (1, 3):
            txt_second(i, j).start()
    for i in range(4):
        txt_second(i, 2).start()
    sib_copy(0).wait_recv()
    img_copy(2).wait_recv()
    img_forward(3).start()
    img_forward(4, 0).start()
    img_copy(6).wait_recv()
    img_forward(5).start()
    img_forward(4, 1).start()
    sib_copy(2).start()
    sib_copy(6).start()
    for k in (1, 7):
        img_copy(k).wait_recv()
        sib_copy(k).start()
    tiles((0,), (0,))
    turn(0)
    for k in (2, 6, 1, 7):
        sib_copy(k).wait_recv()
    tiles((2, 6, 1, 7), (0,))
    for k in (2, 6, 1, 7):
        turn(k)
    txt_quarter(1)
    tiles((0, 2, 6, 1, 7), (1,))
    img_forward(3).wait_recv()
    sib_copy(3).start()
    img_forward(5).wait_recv()
    sib_copy(5).start()
    txt_quarter(3)
    tiles((0, 2, 6, 1, 7), (3,))
    img_forward(4, 0).wait_recv()
    img_forward(4, 1).wait_recv()
    sib_copy(4).start()
    sib_copy(3).wait_recv()
    sib_copy(5).wait_recv()
    tiles((3, 5), (0, 1, 3))
    turn(3)
    turn(5)
    txt_quarter(2)
    tiles((0, 2, 6, 1, 7, 3, 5), (2,))
    for k in (0, 2, 6, 1, 7, 3, 5):
        finish_rows(k)
    sib_copy(4).wait_recv()
    tiles((4,), (0, 1, 3, 2))
    finish_rows(4)
    turn(4)

    def row_msg(d, r):
        return rcopy(msg_r, got_r.at[d * 2 + r], mr_s, mr_r, dev(0, 0, d, r))

    def col_msg(i, j):
        return rcopy(msg_c, got_c.at[j * 4 + i], mc_s, mc_r, dev_ab(i, j))

    def a_msg(i, j):
        return rcopy(out_a, got_a.at[j * 4 + i], la_s, la_r, dev_ab(i, j))

    def b_msg(d, r):
        return rcopy(out_b, got_b.at[d * 2 + r], lb_s, lb_r, dev(0, 0, d, r))

    def combine(parts):
        top = parts[0]
        for p in parts[1:]:
            top = jnp.maximum(top, p)
        total = jnp.exp2(parts[0] - top)
        for p in parts[1:]:
            total = total + jnp.exp2(p - top)
        return top + jnp.log(total) * LOG2E

    for d in (4, 3, 5, 2, 6, 1, 7, 0):
        for r in range(2):
            if (d, r) != (0, 0):
                row_msg(d, r).start()

    for cc in range(COLS // 128):
        lanes = slice(cc * 128, (cc + 1) * 128)
        mt = cm_ref[:, :, lanes].reshape(NZ * 8, 128)
        lt = cl_ref[:, :, lanes].reshape(NZ * 8, 128)
        top = jnp.max(mt, 0, keepdims=True)
        total = jnp.sum(lt * jnp.exp2(mt - top), 0, keepdims=True)
        msg_c[cc : cc + 1, :] = top + jnp.log(total) * LOG2E

    for i, j in reversed(col_peers):
        col_msg(i, j).start()

    drain(got_r.at[pl.ds(1, 15)], mr_r)
    halves = ([], [])
    for d in range(NZ):
        for r in range(2):
            ref = msg_r if (d, r) == (0, 0) else got_r.at[d * 2 + r]
            for rs in range(2):
                v = ref[rs * 8 : rs * 8 + 8, :]
                halves[rs ^ r].append(pltpu.roll(v, d, 0) if d else v)
    lr = [combine(h) for h in halves]
    for k in range(NZ):
        for r in range(2):
            lrb_ref[k * R2 + r * B : k * R2 + (r + 1) * B, :] = (
                jnp.broadcast_to(lr[r][k : k + 1, :], (B, 128)) + 1.0
            ).T

    drain(got_c.at[pl.ds(1, 15)], mc_r)
    jj = lax.broadcasted_iota(jnp.int32, (NX * NY, 128), 0) % NY
    parts = []
    diag = msg_c[16:24, :]
    for a in range(NX):
        for b in range(NY):
            ref = msg_c if (a, b) == (0, 0) else got_c.at[a * NY + b]
            v = ref[0:16, :]
            if (a, b) != (0, 0):
                diag = diag + ref[16:24, :]
            s1, s2 = (4 * a + b) % 16, (4 * a + b + 12) % 16
            if b == 0:
                v = pltpu.roll(v, s1, 0) if s1 else v
            else:
                v = jnp.where(jj >= b, pltpu.roll(v, s1, 0), pltpu.roll(v, s2, 0) if s2 else v)
            parts.append(v)
    lc = combine(parts)
    lc_ref[...] = lc + 1.0

    out_a[...] = (lr[0] + lr[1]) * LN2
    out_b[...] = (lc[0:8] + lc[8:16]) * LN2 - (2.0 * factor) * diag

    def send_shares():
        for i, j in col_peers:
            a_msg(i, j).start()
        for d, r in row_peers:
            b_msg(d, r).start()

    def sib_part(k):
        return rcopy(sib_out.at[k], sib_in.at[k], sb_s, sb_r.at[k], dev(0, 0, 0, 1))

    def far_part(k):
        if k == 3:
            return rcopy(far_out.at[3], mid_in.at[0], fo_s, fo_r.at[3], dev(0, 0, -1, 0))
        if k == 5:
            return rcopy(far_out.at[5], mid_in.at[1], fo_s, fo_r.at[5], dev(0, 0, 1, 0))
        if k == 4:
            rows = pl.ds(0, 64)
            return rcopy(far_out.at[4, rows], mid_in.at[2, rows], fo_s, fo_r.at[4], dev(0, 0, -2, 0))
        if k == 8:
            rows = pl.ds(64, 64)
            return rcopy(far_out.at[4, rows], mid_in.at[2, rows], fo_s, fo_r.at[8], dev(0, 0, 2, 0))
        return rcopy(far_out.at[k], far_in.at[k], fo_s, fo_r.at[k], dev(0, 0, -k, 0))

    def pass_on(k):
        sib_part(k).wait_recv()
        total = keep_i[k] + sib_in[k]
        if k in (2, 6):
            half = 0 if k == 2 else 1
            far_part(3 if k == 2 else 5).wait_recv()
            far_part(4 if k == 2 else 8).wait_recv()
            total = total + mid_in[half].astype(F32)
            h = slice(half * 64, half * 64 + 64)
            far_out[k] = total.astype(BF16)
            far_out[k, h, :] = (total[h] + mid_in[2, h, :].astype(F32)).astype(BF16)
        else:
            far_out[k] = total.astype(BF16)
        far_part(k).start()
        if k == 4:
            far_part(8).start()

    def weigh(k, js):
        rows = slice(k * R2, (k + 1) * R2)
        for j in js:
            for cc in range(j * 4, j * 4 + 4):
                lanes = slice(cc * 128, (cc + 1) * 128)
                s = s_ref[rows, lanes]
                w = jnp.exp2(s - lrb_ref[rows, :]) + jnp.exp2(s - lc_ref[cc : cc + 1, :])
                w_ref[rows, lanes] = w.astype(BF16)

    def txt_part(j):
        return rcopy(t_out.at[j], t_in.at[j], to_s, to_r.at[j], dev_ab(0, -j))

    def txt_part2(i):
        return rcopy(u_out.at[i], u_in.at[i], uo_s, to_r.at[4 + i], dev_ab(-i, 0))

    def third(j):
        return jnp.dot(img_t[...], w_ref[:, j * QC : (j + 1) * QC], preferred_element_type=F32)

    def send_quarter(j):
        t_out[j] = third(j).astype(BF16)
        txt_part(j).start()

    for k in range(NZ):
        weigh(k, (2,))
    send_quarter(2)
    send_shares()
    for k in range(NZ):
        weigh(k, (1,))
    send_quarter(1)
    for k in range(NZ):
        weigh(k, (3,))
    send_quarter(3)

    pairs = (4, 2, 6, 0)
    weigh(4, (0,))
    weigh(5, (0,))
    for n, k in enumerate(pairs):
        if n < 3:
            weigh(pairs[n + 1], (0,))
            weigh(pairs[n + 1] + 1, (0,))
        part = jnp.dot(w_ref[k * R2 : (k + 2) * R2, :], txt_all[...], preferred_element_type=F32)
        for h in (1, 0) if k == 2 else (0, 1):
            keep_i[k + h] = part[h * R2 : h * R2 + B]
            sib_out[k + h] = part[h * R2 + B : (h + 1) * R2]
            sib_part(k + h).start()
        if n == 1:
            pass_on(4)
            pass_on(5)
        if n == 2:
            pass_on(3)
        if n == 3:
            pass_on(7)
    pass_on(1)
    pass_on(2)
    pass_on(6)
    keep_t[...] = third(0)

    drain(got_a.at[pl.ds(1, 15)], la_r)
    drain(got_b.at[pl.ds(1, 15)], lb_r)
    share = out_a[...] + out_b[...]
    for q in range(1, 16):
        share = share + got_a[q] + got_b[q]
    loss_ref[0] = jnp.sum(share) / (2.0 * 256 * B)

    for j in (2, 1, 3):
        txt_part(j).wait_recv()
    for i in (2, 1, 3, 0):
        h = slice(i * B, (i + 1) * B)
        total = keep_t[:, h] + t_in[1, :, h].astype(F32) + t_in[2, :, h].astype(F32) + t_in[3, :, h].astype(F32)
        if i:
            u_out[i] = total.astype(BF16)
            txt_part2(i).start()
        else:
            own_t = total

    sib_part(0).wait_recv()
    total = keep_i[0] + sib_in[0]
    for k in (1, 7, 2, 6):
        far_part(k).wait_recv()
        total = total + far_in[k].astype(F32)
    gi_ref[...] = factor * (total - txt_ref[...].astype(F32))

    for i in (1, 3, 2):
        txt_part2(i).wait_recv()
        own_t = own_t + u_in[i].astype(F32)
    gt_ref[...] = factor * (own_t.T - img_ref[...].astype(F32))

    drain(txt_all.at[pl.ds(0, 15 * B)], ts_s)
    drain(img_all.at[pl.ds(0, 7 * B)], is_s)
    drain(img_all.at[pl.ds(0, 8 * B)], fs_s)
    drain(got_r.at[pl.ds(1, 15)], mr_s)
    drain(got_c.at[pl.ds(1, 15)], mc_s)
    drain(got_a.at[pl.ds(1, 15)], la_s)
    drain(got_b.at[pl.ds(1, 15)], lb_s)
    drain(sib_in, sb_s)
    drain(far_in.at[pl.ds(1, 7)], fo_s)
    drain(t_in.at[pl.ds(1, 3)], to_s)
    drain(u_in.at[pl.ds(1, 3)], uo_s)


def hand_over(loss_in, gi_in, gt_in, loss_ref, gi_ref, gt_ref):
    loss_ref[0] = loss_in[0]
    gi_ref[...] = gi_in[...]
    gt_ref[...] = gt_in[...]


def local(images, texts, logit_scale):
    dma = pltpu.SemaphoreType.DMA
    vm = pltpu.VMEM
    parts = pl.pallas_call(
        kernel,
        out_shape=(
            jax.ShapeDtypeStruct((1,), F32),
            jax.ShapeDtypeStruct((B, E), F32),
            jax.ShapeDtypeStruct((B, E), F32),
        ),
        in_specs=[
            pl.BlockSpec(memory_space=pltpu.SMEM),
            pl.BlockSpec(memory_space=vm),
            pl.BlockSpec(memory_space=vm),
        ],
        out_specs=(
            pl.BlockSpec(memory_space=pltpu.SMEM),
            pl.BlockSpec(memory_space=vm),
            pl.BlockSpec(memory_space=vm),
        ),
        scratch_shapes=[
            vm((ROWS, E), BF16), vm((COLS, E), BF16), vm((E, ROWS), BF16),
            vm((ROWS, COLS), F32), vm((ROWS, COLS), BF16),
            vm((4, ROWS, 128), F32), vm((4, ROWS, 128), F32), vm((NZ, 8, COLS), F32), vm((NZ, 8, COLS), F32),
            vm((ROWS, 128), F32), vm((16, 128), F32),
            vm((16, 128), F32), vm((24, 128), F32), vm((16, 16, 128), F32), vm((16, 24, 128), F32),
            vm((8, 128), F32), vm((8, 128), F32), vm((16, 8, 128), F32), vm((16, 8, 128), F32),
            vm((NZ, B, E), F32), vm((NZ, B, E), F32), vm((NZ, B, E), F32),
            vm((NZ, B, E), BF16), vm((NZ, B, E), BF16), vm((3, B, E), BF16),
            vm((E, QC), F32), vm((4, E, QC), BF16), vm((4, E, QC), BF16), vm((4, E, B), BF16), vm((4, E, B), BF16),
            dma, dma((9,)), dma, dma((NZ,)), dma, dma((7,)),
            dma, dma, dma, dma, dma, dma, dma, dma,
            dma, dma((NZ,)), dma, dma((9,)), dma, dma, dma((8,)),
        ],
        compiler_params=pltpu.CompilerParams(
            collective_id=0, has_side_effects=True, vmem_limit_bytes=56 * 1024 * 1024
        ),
        cost_estimate=pl.CostEstimate(
            flops=6 * ROWS * COLS * E, bytes_accessed=8 * B * E, transcendentals=4 * ROWS * COLS
        ),
    )(logit_scale, images, texts)
    return pl.pallas_call(
        hand_over,
        out_shape=(
            jax.ShapeDtypeStruct((1,), F32),
            jax.ShapeDtypeStruct((B, E), F32),
            jax.ShapeDtypeStruct((B, E), F32),
        ),
        in_specs=[pl.BlockSpec(memory_space=pltpu.SMEM), pl.BlockSpec(memory_space=vm), pl.BlockSpec(memory_space=vm)],
        out_specs=(
            pl.BlockSpec(memory_space=pltpu.SMEM), pl.BlockSpec(memory_space=vm), pl.BlockSpec(memory_space=vm)
        ),
    )(*parts)


def solution(mesh):
    spec = P(("outer", "inner"), None)
    return jax.shard_map(
        local, mesh=mesh, in_specs=(spec, spec, P()), out_specs=(P(), spec, spec), check_vma=False
    )
```

```python
import math

import jax
import jax.numpy as jnp
from jax import lax
from jax.experimental import pallas as pl
from jax.experimental.pallas import tpu as pltpu
from jax.sharding import PartitionSpec as P

MESH = pl.DeviceIdType.MESH
F32 = jnp.float32
BF16 = jnp.bfloat16
B = 128
E = 384
NX, NY, NZ = 4, 4, 8
ROWS = NZ * 2 * B
COLS = NX * NY * B
R2 = 2 * B
QC = 4 * B
LOG2E = math.log2(math.e)
LN2 = math.log(2.0)


def nt(a, b):
    return lax.dot_general(a, b, (((1,), (1,)), ((), ())), preferred_element_type=F32)


def kernel(
    scale_ref, img_ref, txt_ref, loss_ref, gi_ref, gt_ref,
    img_all, txt_all, img_t, s_ref, w_ref,
    rm_ref, rl_ref, cm_ref, cl_ref, lrb_ref, lc_ref,
    msg_r, msg_c, got_r, got_c, out_a, out_b, got_a, got_b,
    keep_i, sib_out, sib_in, far_out, far_in, mid_in, keep_t, t_out, t_in, u_out, u_in,
    is_s, is_r, fs_s, fs_r, ts_s, ts_r, mr_s, mr_r, mc_s, mc_r,
    la_s, la_r, lb_s, lb_r, sb_s, sb_r, fo_s, fo_r, to_s, uo_s, to_r,
):
    outer, inner = lax.axis_index("outer"), lax.axis_index("inner")
    c = outer % 2
    x = (outer // 2) % NX
    y = (outer // (2 * NX)) * 2 + inner // NZ
    z = inner % NZ
    factor = scale_ref[0]
    f2 = factor * LOG2E

    def dev(dx, dy, dz, dc):
        xx, yy, zz = (x + dx + NX) % NX, (y + dy + NY) % NY, (z + dz + NZ) % NZ
        cc = (c + dc) % 2
        return ((yy // 2) * (2 * NX) + xx * 2 + cc, (yy % 2) * NZ + zz)

    def dev_ab(da, db):
        return dev(jnp.where(c == 0, da, db), jnp.where(c == 0, db, da), 0, 0)

    def rcopy(src, dst, ss, rs, to):
        return pltpu.make_async_remote_copy(
            src_ref=src, dst_ref=dst, send_sem=ss, recv_sem=rs, device_id=to, device_id_type=MESH
        )

    def drain(ref, sem):
        pltpu.make_async_copy(ref, ref, sem).wait()

    barrier = pltpu.get_barrier_semaphore()
    row_peers = [(d, r) for d in range(NZ) for r in range(2) if (d, r) != (0, 0)]
    col_peers = [(i, j) for i in range(NX) for j in range(NY) if (i, j) != (0, 0)]
    near = [dev_ab(i, 0) for i in (1, 3, 2)] + [dev_ab(0, j) for j in (1, 3, 2)]
    near += [dev(0, 0, d, 0) for d in (1, 7, 2, 6)] + [dev(0, 0, 0, 1)]
    for to in near:
        pl.semaphore_signal(barrier, inc=1, device_id=to, device_id_type=MESH)
    pl.semaphore_wait(barrier, len(near))

    def img_rows(k, h=None):
        return img_all.at[pl.ds(k * R2, B)] if h is None else img_all.at[pl.ds(k * R2 + h * 64, 64)]

    def img_copy(k):
        return rcopy(img_ref, img_rows(k), is_s, is_r.at[k], dev(0, 0, k, 0))

    def img_forward(k, h=None):
        if k == 3:
            return rcopy(img_rows(2), img_rows(3), is_s, is_r.at[3], dev(0, 0, 1, 0))
        if k == 5:
            return rcopy(img_rows(6), img_rows(5), is_s, is_r.at[5], dev(0, 0, -1, 0))
        if h == 0:
            return rcopy(img_rows(2, 0), img_rows(4, 0), is_s, is_r.at[4], dev(0, 0, 2, 0))
        return rcopy(img_rows(6, 1), img_rows(4, 1), is_s, is_r.at[8], dev(0, 0, -2, 0))

    def sib_copy(k):
        return rcopy(img_rows(k), img_all.at[pl.ds(k * R2 + B, B)], fs_s, fs_r.at[k], dev(0, 0, 0, 1))

    def txt_first(i):
        return rcopy(txt_ref, txt_all.at[pl.ds(i * B, B)], ts_s, ts_r.at[i], dev_ab(i, 0))

    def txt_second(i, j):
        return rcopy(
            txt_all.at[pl.ds(i * B, B)], txt_all.at[pl.ds((j * 4 + i) * B, B)], ts_s, ts_r.at[3 + j], dev_ab(0, j)
        )

    def txt_quarter(j):
        drain(txt_all.at[pl.ds(j * QC, QC)], ts_r.at[3 + j])

    img_all[0:B, :] = img_ref[...]
    txt_all[0:B, :] = txt_ref[...]
    for i in (1, 3, 2):
        txt_first(i).start()
    for k in (2, 6, 1, 7):
        img_copy(k).start()
    for j in (1, 3):
        txt_second(0, j).start()
    sib_copy(0).start()

    prod = img_ref[...].astype(F32) * txt_ref[...].astype(F32)
    prod = prod[:, 0:128] + prod[:, 128:256] + prod[:, 256:384]
    msg_c[16:24, :] = jnp.sum(prod.reshape(B // 8, 8, 128), 0)

    def tile(k, j):
        row0 = k * R2
        block = img_all[row0 : row0 + R2, :]
        for cc in range(j * 2, j * 2 + 2):
            s = nt(block, txt_all[cc * 256 : (cc + 1) * 256, :]) * f2
            s_ref[row0 : row0 + R2, cc * 256 : (cc + 1) * 256] = s
        for cc in range(j * 4, j * 4 + 4):
            lanes = slice(cc * 128, (cc + 1) * 128)
            slab = s_ref[row0 : row0 + R2, lanes].reshape(R2 // 8, 8, 128)
            top = jnp.max(slab, 0)
            cm_ref[k, :, lanes] = top
            cl_ref[k, :, lanes] = jnp.sum(jnp.exp2(slab - top[None]), 0)
        for rr in range(R2 // 32):
            rows = slice(row0 + rr * 32, row0 + rr * 32 + 32)
            parts = [s_ref[rows, cc * 128 : (cc + 1) * 128] for cc in range(j * 4, j * 4 + 4)]
            top = jnp.maximum(jnp.maximum(parts[0], parts[1]), jnp.maximum(parts[2], parts[3]))
            e = [jnp.exp2(p - top) for p in parts]
            rm_ref[j, rows, :] = top
            rl_ref[j, rows, :] = (e[0] + e[1]) + (e[2] + e[3])

    def tiles(ks, js):
        for j in js:
            for k in ks:
                tile(k, j)

    def turn(k):
        img_t[:, k * R2 : (k + 1) * R2] = img_all[k * R2 : (k + 1) * R2, :].T

    def finish_rows(k):
        for r in range(2):
            rows = slice(k * R2 + r * B, k * R2 + r * B + B)
            m = [rm_ref[j, rows, :] for j in range(4)]
            top = jnp.maximum(jnp.maximum(m[0], m[1]), jnp.maximum(m[2], m[3]))
            e = [rl_ref[j, rows, :] * jnp.exp2(m[j] - top) for j in range(4)]
            v = (top + jnp.log((e[0] + e[1]) + (e[2] + e[3])) * LOG2E).T
            top = jnp.max(v, 0, keepdims=True)
            q = r * NZ + k
            msg_r[q : q + 1, :] = top + jnp.log(jnp.sum(jnp.exp2(v - top), 0, keepdims=True)) * LOG2E

    for i in (1, 3, 2):
        txt_first(i).wait_recv()
        for j in (1, 3):
            txt_second(i, j).start()
    for i in range(4):
        txt_second(i, 2).start()
    sib_copy(0).wait_recv()
    img_copy(2).wait_recv()
    img_forward(3).start()
    img_forward(4, 0).start()
    img_copy(6).wait_recv()
    img_forward(5).start()
    img_forward(4, 1).start()
    sib_copy(2).start()
    sib_copy(6).start()
    for k in (1, 7):
        img_copy(k).wait_recv()
        sib_copy(k).start()
    tiles((0,), (0,))
    turn(0)
    for k in (2, 6, 1, 7):
        sib_copy(k).wait_recv()
    tiles((2, 6, 1, 7), (0,))
    for k in (2, 6, 1, 7):
        turn(k)
    txt_quarter(1)
    tiles((0, 2, 6, 1, 7), (1,))
    img_forward(3).wait_recv()
    sib_copy(3).start()
    img_forward(5).wait_recv()
    sib_copy(5).start()
    txt_quarter(3)
    tiles((0, 2, 6, 1, 7), (3,))
    img_forward(4, 0).wait_recv()
    img_forward(4, 1).wait_recv()
    sib_copy(4).start()
    sib_copy(3).wait_recv()
    sib_copy(5).wait_recv()
    tiles((3, 5), (0, 1, 3))
    turn(3)
    turn(5)
    txt_quarter(2)
    tiles((0, 2, 6, 1, 7, 3, 5), (2,))
    for k in (0, 2, 6, 1, 7, 3, 5):
        finish_rows(k)
    sib_copy(4).wait_recv()
    tiles((4,), (0, 1, 3, 2))
    finish_rows(4)
    turn(4)

    def row_msg(d, r):
        return rcopy(msg_r, got_r.at[d * 2 + r], mr_s, mr_r, dev(0, 0, d, r))

    def col_msg(i, j):
        return rcopy(msg_c, got_c.at[j * 4 + i], mc_s, mc_r, dev_ab(i, j))

    def a_msg(i, j):
        return rcopy(out_a, got_a.at[j * 4 + i], la_s, la_r, dev_ab(i, j))

    def b_msg(d, r):
        return rcopy(out_b, got_b.at[d * 2 + r], lb_s, lb_r, dev(0, 0, d, r))

    def combine(parts):
        top = parts[0]
        for p in parts[1:]:
            top = jnp.maximum(top, p)
        total = jnp.exp2(parts[0] - top)
        for p in parts[1:]:
            total = total + jnp.exp2(p - top)
        return top + jnp.log(total) * LOG2E

    for d in (4, 3, 5, 2, 6, 1, 7, 0):
        for r in range(2):
            if (d, r) != (0, 0):
                row_msg(d, r).start()

    for cc in range(COLS // 128):
        lanes = slice(cc * 128, (cc + 1) * 128)
        mt = cm_ref[:, :, lanes].reshape(NZ * 8, 128)
        lt = cl_ref[:, :, lanes].reshape(NZ * 8, 128)
        top = jnp.max(mt, 0, keepdims=True)
        total = jnp.sum(lt * jnp.exp2(mt - top), 0, keepdims=True)
        msg_c[cc : cc + 1, :] = top + jnp.log(total) * LOG2E

    for i, j in reversed(col_peers):
        col_msg(i, j).start()

    drain(got_r.at[pl.ds(1, 15)], mr_r)
    halves = ([], [])
    for d in range(NZ):
        for r in range(2):
            ref = msg_r if (d, r) == (0, 0) else got_r.at[d * 2 + r]
            for rs in range(2):
                v = ref[rs * 8 : rs * 8 + 8, :]
                halves[rs ^ r].append(pltpu.roll(v, d, 0) if d else v)
    lr = [combine(h) for h in halves]
    for k in range(NZ):
        for r in range(2):
            lrb_ref[k * R2 + r * B : k * R2 + (r + 1) * B, :] = (
                jnp.broadcast_to(lr[r][k : k + 1, :], (B, 128)) + 1.0
            ).T

    drain(got_c.at[pl.ds(1, 15)], mc_r)
    jj = lax.broadcasted_iota(jnp.int32, (NX * NY, 128), 0) % NY
    parts = []
    diag = msg_c[16:24, :]
    for a in range(NX):
        for b in range(NY):
            ref = msg_c if (a, b) == (0, 0) else got_c.at[a * NY + b]
            v = ref[0:16, :]
            if (a, b) != (0, 0):
                diag = diag + ref[16:24, :]
            s1, s2 = (4 * a + b) % 16, (4 * a + b + 12) % 16
            if b == 0:
                v = pltpu.roll(v, s1, 0) if s1 else v
            else:
                v = jnp.where(jj >= b, pltpu.roll(v, s1, 0), pltpu.roll(v, s2, 0) if s2 else v)
            parts.append(v)
    lc = combine(parts)
    lc_ref[...] = lc + 1.0

    out_a[...] = (lr[0] + lr[1]) * LN2
    out_b[...] = (lc[0:8] + lc[8:16]) * LN2 - (2.0 * factor) * diag

    def send_shares():
        for i, j in col_peers:
            a_msg(i, j).start()
        for d, r in row_peers:
            b_msg(d, r).start()

    def sib_part(k):
        return rcopy(sib_out.at[k], sib_in.at[k], sb_s, sb_r.at[k], dev(0, 0, 0, 1))

    def far_part(k):
        if k == 3:
            return rcopy(far_out.at[3], mid_in.at[0], fo_s, fo_r.at[3], dev(0, 0, -1, 0))
        if k == 5:
            return rcopy(far_out.at[5], mid_in.at[1], fo_s, fo_r.at[5], dev(0, 0, 1, 0))
        if k == 4:
            rows = pl.ds(0, 64)
            return rcopy(far_out.at[4, rows], mid_in.at[2, rows], fo_s, fo_r.at[4], dev(0, 0, -2, 0))
        if k == 8:
            rows = pl.ds(64, 64)
            return rcopy(far_out.at[4, rows], mid_in.at[2, rows], fo_s, fo_r.at[8], dev(0, 0, 2, 0))
        return rcopy(far_out.at[k], far_in.at[k], fo_s, fo_r.at[k], dev(0, 0, -k, 0))

    def pass_on(k):
        sib_part(k).wait_recv()
        total = keep_i[k] + sib_in[k]
        if k in (2, 6):
            half = 0 if k == 2 else 1
            far_part(3 if k == 2 else 5).wait_recv()
            far_part(4 if k == 2 else 8).wait_recv()
            total = total + mid_in[half].astype(F32)
            h = slice(half * 64, half * 64 + 64)
            far_out[k] = total.astype(BF16)
            far_out[k, h, :] = (total[h] + mid_in[2, h, :].astype(F32)).astype(BF16)
        else:
            far_out[k] = total.astype(BF16)
        far_part(k).start()
        if k == 4:
            far_part(8).start()

    def weigh(k, js):
        rows = slice(k * R2, (k + 1) * R2)
        for j in js:
            for cc in range(j * 4, j * 4 + 4):
                lanes = slice(cc * 128, (cc + 1) * 128)
                s = s_ref[rows, lanes]
                w = jnp.exp2(s - lrb_ref[rows, :]) + jnp.exp2(s - lc_ref[cc : cc + 1, :])
                w_ref[rows, lanes] = w.astype(BF16)

    def txt_part(j):
        return rcopy(t_out.at[j], t_in.at[j], to_s, to_r.at[j], dev_ab(0, -j))

    def txt_part2(i):
        return rcopy(u_out.at[i], u_in.at[i], uo_s, to_r.at[4 + i], dev_ab(-i, 0))

    def third(j):
        return jnp.dot(img_t[...], w_ref[:, j * QC : (j + 1) * QC], preferred_element_type=F32)

    def send_quarter(j):
        t_out[j] = third(j).astype(BF16)
        txt_part(j).start()

    for k in range(NZ):
        weigh(k, (2,))
    send_quarter(2)
    send_shares()
    for k in range(NZ):
        weigh(k, (1,))
    send_quarter(1)
    for k in range(NZ):
        weigh(k, (3,))
    send_quarter(3)

    pairs = (4, 2, 6, 0)
    weigh(4, (0,))
    weigh(5, (0,))
    for n, k in enumerate(pairs):
        if n < 3:
            weigh(pairs[n + 1], (0,))
            weigh(pairs[n + 1] + 1, (0,))
        part = jnp.dot(w_ref[k * R2 : (k + 2) * R2, :], txt_all[...], preferred_element_type=F32)
        for h in (1, 0) if k == 2 else (0, 1):
            keep_i[k + h] = part[h * R2 : h * R2 + B]
            sib_out[k + h] = part[h * R2 + B : (h + 1) * R2]
            sib_part(k + h).start()
        if n == 1:
            pass_on(4)
            pass_on(5)
        if n == 2:
            pass_on(3)
        if n == 3:
            pass_on(7)
    pass_on(1)
    pass_on(2)
    pass_on(6)
    keep_t[...] = third(0)

    drain(got_a.at[pl.ds(1, 15)], la_r)
    drain(got_b.at[pl.ds(1, 15)], lb_r)
    share = out_a[...] + out_b[...]
    for q in range(1, 16):
        share = share + got_a[q] + got_b[q]
    loss_ref[0] = jnp.sum(share) / (2.0 * 256 * B)

    for j in (2, 1, 3):
        txt_part(j).wait_recv()
    for i in (2, 1, 3, 0):
        h = slice(i * B, (i + 1) * B)
        total = keep_t[:, h] + t_in[1, :, h].astype(F32) + t_in[2, :, h].astype(F32) + t_in[3, :, h].astype(F32)
        if i:
            u_out[i] = total.astype(BF16)
            txt_part2(i).start()
        else:
            own_t = total

    sib_part(0).wait_recv()
    total = keep_i[0] + sib_in[0]
    for k in (1, 7, 2, 6):
        far_part(k).wait_recv()
        total = total + far_in[k].astype(F32)
    gi_ref[...] = factor * (total - txt_ref[...].astype(F32))

    for i in (1, 3, 2):
        txt_part2(i).wait_recv()
        own_t = own_t + u_in[i].astype(F32)
    gt_ref[...] = factor * (own_t.T - img_ref[...].astype(F32))

    drain(txt_all.at[pl.ds(0, 15 * B)], ts_s)
    drain(img_all.at[pl.ds(0, 7 * B)], is_s)
    drain(img_all.at[pl.ds(0, 8 * B)], fs_s)
    drain(got_r.at[pl.ds(1, 15)], mr_s)
    drain(got_c.at[pl.ds(1, 15)], mc_s)
    drain(got_a.at[pl.ds(1, 15)], la_s)
    drain(got_b.at[pl.ds(1, 15)], lb_s)
    drain(sib_in, sb_s)
    drain(far_in.at[pl.ds(1, 7)], fo_s)
    drain(t_in.at[pl.ds(1, 3)], to_s)
    drain(u_in.at[pl.ds(1, 3)], uo_s)


def hand_over(loss_in, gi_in, gt_in, loss_ref, gi_ref, gt_ref):
    loss_ref[0] = loss_in[0]
    gi_ref[...] = gi_in[...]
    gt_ref[...] = gt_in[...]


def local(images, texts, logit_scale):
    dma = pltpu.SemaphoreType.DMA
    vm = pltpu.VMEM
    parts = pl.pallas_call(
        kernel,
        out_shape=(
            jax.ShapeDtypeStruct((1,), F32),
            jax.ShapeDtypeStruct((B, E), F32),
            jax.ShapeDtypeStruct((B, E), F32),
        ),
        in_specs=[
            pl.BlockSpec(memory_space=pltpu.SMEM),
            pl.BlockSpec(memory_space=vm),
            pl.BlockSpec(memory_space=vm),
        ],
        out_specs=(
            pl.BlockSpec(memory_space=pltpu.SMEM),
            pl.BlockSpec(memory_space=vm),
            pl.BlockSpec(memory_space=vm),
        ),
        scratch_shapes=[
            vm((ROWS, E), BF16), vm((COLS, E), BF16), vm((E, ROWS), BF16),
            vm((ROWS, COLS), F32), vm((ROWS, COLS), BF16),
            vm((4, ROWS, 128), F32), vm((4, ROWS, 128), F32), vm((NZ, 8, COLS), F32), vm((NZ, 8, COLS), F32),
            vm((ROWS, 128), F32), vm((16, 128), F32),
            vm((16, 128), F32), vm((24, 128), F32), vm((16, 16, 128), F32), vm((16, 24, 128), F32),
            vm((8, 128), F32), vm((8, 128), F32), vm((16, 8, 128), F32), vm((16, 8, 128), F32),
            vm((NZ, B, E), F32), vm((NZ, B, E), F32), vm((NZ, B, E), F32),
            vm((NZ, B, E), BF16), vm((NZ, B, E), BF16), vm((3, B, E), BF16),
            vm((E, QC), F32), vm((4, E, QC), BF16), vm((4, E, QC), BF16), vm((4, E, B), BF16), vm((4, E, B), BF16),
            dma, dma((9,)), dma, dma((NZ,)), dma, dma((7,)),
            dma, dma, dma, dma, dma, dma, dma, dma,
            dma, dma((NZ,)), dma, dma((9,)), dma, dma, dma((8,)),
        ],
        compiler_params=pltpu.CompilerParams(
            collective_id=0, has_side_effects=True, vmem_limit_bytes=56 * 1024 * 1024
        ),
        cost_estimate=pl.CostEstimate(
            flops=6 * ROWS * COLS * E, bytes_accessed=8 * B * E, transcendentals=4 * ROWS * COLS
        ),
    )(logit_scale, images, texts)
    return pl.pallas_call(
        hand_over,
        out_shape=(
            jax.ShapeDtypeStruct((1,), F32),
            jax.ShapeDtypeStruct((B, E), F32),
            jax.ShapeDtypeStruct((B, E), F32),
        ),
        in_specs=[pl.BlockSpec(memory_space=pltpu.SMEM), pl.BlockSpec(memory_space=vm), pl.BlockSpec(memory_space=vm)],
        out_specs=(
            pl.BlockSpec(memory_space=pltpu.SMEM), pl.BlockSpec(memory_space=vm), pl.BlockSpec(memory_space=vm)
        ),
    )(*parts)


def solution(mesh):
    spec = P(("outer", "inner"), None)
    return jax.shard_map(
        local, mesh=mesh, in_specs=(spec, spec, P()), out_specs=(P(), spec, spec), check_vma=False
    )
```
